512 devices in a mesh: dp: 32 (over y, z_lo), seq: 16 (over x, z_hi, core).
Axes of the slice: x: 4, y: 8, z: 8 (z_hi: 2, z_lo: 4; z = z_hi * 4 + z_lo), core: 2. Of those that a mesh axis runs over, the one named last changes fastest.
Arguments:
- queries: bfloat16 [32, 2048, 768], P('dp', 'seq'), may hold values from -8 to 8
- keys: bfloat16 [32, 2048, 768], P('dp', 'seq'), may hold values from -8 to 8
- values: bfloat16 [32, 2048, 768], P('dp', 'seq'), may hold values from -6 to 6
- cotangent: bfloat16 [32, 2048, 768], P('dp', 'seq'), may hold values from -6 to 6
- pair: bfloat16 [32, 128, 128, 128], P('dp', 'seq'), may hold values from -6 to 6
- pair_weight: float32 [128, 4], replicated, may hold values from -0.5 to 0.5
Outputs:
- attended: bfloat16 [32, 2048, 768], P('dp', 'seq')
- grad_queries: bfloat16 [32, 2048, 768], P('dp', 'seq')
- grad_keys: bfloat16 [32, 2048, 768], P('dp', 'seq')
- grad_values: bfloat16 [32, 2048, 768], P('dp', 'seq')
- grad_pair: bfloat16 [32, 128, 128, 128], P('dp', 'seq')
- grad_weight: float32 [128, 4], replicated
The draws below stay inside these ranges and needn't reach their ends.
All inputs are finite; a program needn't handle non-finite values.
Results may differ from the reference program's by a relative error of at most 0.023.
Values may be sent and summed in bfloat16 or wider, within the bound.
No kernel may reach another device: no remote copies, remote signals or barrier semaphores. Data moves between devices by JAX's collectives and lax.ppermute only.
A program may use at most 64 MiB of HBM per device.

```python
import jax
import jax.numpy as jnp
from jax import lax

HEADS = 4
HEAD_DIM = 192
CHANNELS = 128
POOL = 16
SEQ = 2048
PAIRS = 128
EXAMPLES = 32


def draw_queries(key, part):
    key = jax.random.fold_in(key, 1)
    base = jnp.clip(jax.random.normal(key, (EXAMPLES, SEQ, HEADS * HEAD_DIM), jnp.float32), -6.0, 6.0)
    return base.astype(jnp.bfloat16)


def draw_keys(key, part):
    key = jax.random.fold_in(key, 2)
    base = jnp.clip(jax.random.normal(key, (EXAMPLES, SEQ, HEADS * HEAD_DIM), jnp.float32), -6.0, 6.0)
    return base.astype(jnp.bfloat16)


def levels(own_key, extent, pieces, smallest, largest):
    factor_of, own = 1.0, jax.random.fold_in(own_key, 6)
    for dim, blocks in pieces:
        heights = jnp.exp(jax.random.uniform(jax.random.fold_in(own, dim), (blocks,), jnp.float32, smallest / len(pieces), largest / len(pieces)))
        factor_of = factor_of * jnp.repeat(heights, extent[dim] // blocks).reshape([-1 if axis == dim else 1 for axis in range(len(extent))])
    return factor_of


def centred(key, shape, scale, limit, cuts=(), kind=jnp.bfloat16):
    factor_of = levels(key, shape, cuts, -0.22, 0.18) if cuts else 1.0
    entries = jax.random.normal(key, shape, jnp.float32) * scale * factor_of
    return jnp.minimum(jnp.maximum(entries, -limit), limit).astype(kind)


def setup_inputs(seed: int = 0) -> dict:
    arg_keys = jax.random.split(jax.random.key(seed), 7)
    queries = draw_queries(jax.random.fold_in(arg_keys[6], 71), 0)
    keys = draw_keys(jax.random.fold_in(arg_keys[6], 71), 0)
    values = centred(arg_keys[2], (EXAMPLES, SEQ, HEADS * HEAD_DIM), 1.0, 6.0, ((0, 32), (1, 16)))
    cotangent = centred(arg_keys[3], (EXAMPLES, SEQ, HEADS * HEAD_DIM), 1.0, 6.0, ((0, 32), (1, 16)))
    pair = centred(arg_keys[4], (EXAMPLES, PAIRS, PAIRS, CHANNELS), 1.0, 6.0, ((0, 32), (1, 16)))
    pair_weight = centred(arg_keys[5], (CHANNELS, HEADS), CHANNELS ** -0.5, 0.5, (), jnp.float32)
    return {"queries": queries, "keys": keys, "values": values, "cotangent": cotangent, "pair": pair, "pair_weight": pair_weight}


def one_example(args):
    queries, keys, values, cotangent, pair, pair_weight = args
    length = queries.shape[0]
    scale = HEAD_DIM ** -0.5
    qf = queries.astype(jnp.float32).reshape(length, HEADS, HEAD_DIM)
    kf = keys.astype(jnp.float32).reshape(length, HEADS, HEAD_DIM)
    vf = values.astype(jnp.float32).reshape(length, HEADS, HEAD_DIM)
    cf = cotangent.astype(jnp.float32).reshape(length, HEADS, HEAD_DIM)
    pair_f = pair.astype(jnp.float32)
    bias = jnp.einsum('ijc,ch->hij', pair_f, pair_weight, precision=lax.Precision.HIGHEST)
    bias_up = jnp.repeat(jnp.repeat(bias, POOL, axis=1), POOL, axis=2)
    scores = jnp.einsum('qhe,khe->hqk', qf, kf) * scale + bias_up
    rowmax = jnp.max(scores, axis=-1, keepdims=True)
    total = jnp.sum(jnp.exp(scores - rowmax), axis=-1, keepdims=True)
    lse = rowmax + jnp.log(total)
    weights = jnp.exp(scores - rowmax).astype(jnp.bfloat16).astype(jnp.float32)
    summed = jnp.einsum('hqk,khe->hqe', weights, vf) / total
    attended = jnp.transpose(summed, (1, 0, 2)).astype(jnp.bfloat16)
    probs = jnp.exp(scores - lse)
    probs_low = probs.astype(jnp.bfloat16).astype(jnp.float32)
    delta = jnp.einsum('qhe,qhe->hq', cf, attended.astype(jnp.float32))
    grad_values = jnp.einsum('hqk,qhe->khe', probs_low, cf).astype(jnp.bfloat16)
    dprod = jnp.einsum('qhe,khe->hqk', cf, vf)
    dscores = probs * (dprod - delta[:, :, None])
    dscores_low = dscores.astype(jnp.bfloat16).astype(jnp.float32)
    grad_queries = (jnp.einsum('hqk,khe->qhe', dscores_low, kf) * scale).astype(jnp.bfloat16)
    grad_keys = (jnp.einsum('hqk,qhe->khe', dscores_low, qf) * scale).astype(jnp.bfloat16)
    npair = length // POOL
    grad_bias = dscores.reshape(HEADS, npair, POOL, npair, POOL).sum(axis=(2, 4))
    grad_pair = jnp.einsum('hij,ch->ijc', grad_bias, pair_weight, precision=lax.Precision.HIGHEST).astype(jnp.bfloat16)
    grad_weight = jnp.einsum('ijc,hij->ch', pair_f, grad_bias, precision=lax.Precision.HIGHEST)
    width = HEADS * HEAD_DIM
    return (attended.reshape(length, width), grad_queries.reshape(length, width),
            grad_keys.reshape(length, width), grad_values.reshape(length, width),
            grad_pair, grad_weight)


def reference(queries, keys, values, cotangent, pair, pair_weight):
    count = queries.shape[0]
    weight_rep = jnp.broadcast_to(pair_weight, (count,) + pair_weight.shape)
    results = lax.map(one_example, (queries, keys, values, cotangent, pair, weight_rep))
    attended, grad_queries, grad_keys, grad_values, grad_pair, grad_weight = results
    return (attended, grad_queries, grad_keys, grad_values, grad_pair, jnp.sum(grad_weight, axis=0))
```

```python
import functools
import math

import jax
import jax.numpy as jnp
from jax import lax
from jax.experimental import pallas as pl
from jax.experimental.pallas import tpu as pltpu
from jax.sharding import PartitionSpec as P

HEADS = 4
HDIM = 192
TOK = 128
POOL = 16
PROW = TOK // POOL
PAIRS = 128
XS = 4
ZS = 2
CS = 2
QROWS = XS * TOK
KROWS = XS * ZS * CS * TOK
BLOCK = 256
SCALE = HDIM ** (-0.5)
LOG2E = 1.0 / math.log(2.0)
BF = jnp.bfloat16
F32 = jnp.float32
VMEM = pl.BlockSpec(memory_space=pltpu.VMEM)
SMEM = pl.BlockSpec(memory_space=pltpu.SMEM)

FULL_TILE = (0, 2, 3, 5)
HALF_TILE = (1, 1, 4, 4)


def nn(a, b):
    return lax.dot_general(a, b, (((1,), (0,)), ((), ())), preferred_element_type=F32)


def nt(a, b):
    return lax.dot_general(a, b, (((1,), (1,)), ((), ())), preferred_element_type=F32)


def tn(a, b):
    return lax.dot_general(a, b, (((0,), (0,)), ((), ())), preferred_element_type=F32)


def roll_half(x):
    return pltpu.roll(x, 64, 1)


def low_lanes(rows):
    return lax.broadcasted_iota(jnp.int32, (rows, 128), 1) < 64


def split2(x):
    hi = x.astype(BF)
    return hi, (x - hi.astype(F32)).astype(BF)


def split3(x):
    hi = x.astype(BF)
    rest = x - hi.astype(F32)
    mid = rest.astype(BF)
    return hi, mid, (rest - mid.astype(F32)).astype(BF)


def pack_heads(ref):
    low = low_lanes(64)
    for pair in range(2):
        tile = ref[:, (3 * pair + 1) * 128 : (3 * pair + 2) * 128].astype(F32)
        top, bottom = tile[:64], tile[64:]
        even = jnp.where(low, top, roll_half(bottom)).astype(BF)
        odd = jnp.where(low, roll_half(top), bottom).astype(BF)
        for parity, half in ((0, even), (1, odd)):
            head = 2 * pair + parity
            full = FULL_TILE[head]
            yield head, ref[:, full * 128 : (full + 1) * 128], half


def pack_kernel(q_ref, k_ref, v_ref, c_ref, pair_ref, wt_ref, kv_ref, qd_ref):
    for base, ref in ((0, k_ref), (1, v_ref)):
        for head, full, half in pack_heads(ref):
            for zs in range(ZS):
                slot = head * ZS + zs
                kv_ref[slot, base * 128 : (base + 1) * 128, :] = full
                kv_ref[slot, 256 + base * 64 : 320 + base * 64, :] = half
    for base, ref in ((0, q_ref), (1, c_ref)):
        for head, full, half in pack_heads(ref):
            qd_ref[head, base * 128 : (base + 1) * 128, :] = full
            qd_ref[head, 256 + base * 64 : 320 + base * 64, :] = half
    parts = jnp.concatenate([p.astype(F32) for p in split3(wt_ref[...])], axis=0).astype(BF)
    pair = pair_ref[...].reshape(PROW * PAIRS, 128)
    prod = nt(parts, pair)
    bias = (prod[0:8] + (prod[8:16] + prod[16:24])) * (1.0 / SCALE)
    for head in range(HEADS):
        rows = jnp.concatenate(
            [bias[head : head + 1, i * 128 : (i + 1) * 128] for i in range(PROW)], axis=0
        )
        hi = rows.astype(BF).astype(F32)
        qd_ref[head, 384:400, :] = jnp.concatenate([hi, rows - hi], axis=0).astype(BF)


def unpack(full, half, rows_low):
    half = half.astype(F32)
    top = jnp.where(rows_low, half, 0.0)
    bottom = jnp.where(rows_low, roll_half(half), 0.0)
    other = jnp.concatenate([top, bottom], axis=0).astype(BF)
    return full, other


def pack_out(block):
    rest = block[:, 128:]
    return block[:, :128].astype(BF), (rest[:64] + roll_half(rest[64:])).astype(BF)


def attn_kernel(
    core_ref, qd_ref, kvo_ref, kvx_ref, oq_ref, dko_ref, dkx_ref,
    ke, vs, qe, cs, st, ot, dqt, pool,
):
    core = core_ref[0]
    low = low_lanes(64)
    for half, ref in ((0, kvo_ref), (1, kvx_ref)):
        for m in range(8):
            base = half * 1024 + m * 128
            full, other = unpack(ref[m, 0:128, :], ref[m, 256:320, :], low)
            ke[base : base + 128, 0:128] = full
            ke[base : base + 128, 128:256] = other
            full, other = unpack(ref[m, 128:256, :], ref[m, 320:384, :], low)
            vs[base : base + 128, 0:128] = full
            vs[base : base + 128, 128:256] = other
        row = lax.broadcasted_iota(jnp.int32, (1024, 128), 0)
        col = lax.broadcasted_iota(jnp.int32, (1024, 128), 1)
        mine = core if half == 0 else 1 - core
        cell = lax.shift_right_logical(row, 7) * 16 + mine * 8 + (lax.shift_right_logical(row, 4) & 7)
        table = jnp.where(cell == col, 1.0, 0.0).astype(BF)
        ke[half * 1024 : (half + 1) * 1024, 256:384] = table
        ke[half * 1024 : (half + 1) * 1024, 384:512] = table
    for x in range(XS):
        base = x * 128
        full, other = unpack(qd_ref[x, 0:128, :], qd_ref[x, 256:320, :], low)
        qe[base : base + 128, 0:128] = full
        qe[base : base + 128, 128:256] = other
        full, other = unpack(qd_ref[x, 128:256, :], qd_ref[x, 320:384, :], low)
        cs[base : base + 128, 0:128] = full
        cs[base : base + 128, 128:256] = other
        rows = qd_ref[x, 384:400, :].astype(F32)
        for part in range(2):
            wide = jnp.broadcast_to(rows[part * 8 : part * 8 + 8, None, :], (8, POOL, 128))
            qe[base : base + 128, 256 + part * 128 : 384 + part * 128] = wide.reshape(128, 128).astype(BF)

    steps = KROWS // BLOCK

    def scores(b, top):
        at = pl.ds(pl.multiple_of(b * BLOCK, BLOCK), BLOCK)
        s = nt(ke[at, :], qe[...])
        st[at, :] = s
        return jnp.maximum(top, jnp.max(s.reshape(BLOCK // 8, 8, QROWS), axis=0))

    top = lax.fori_loop(0, steps, scores, jnp.full((8, QROWS), -jnp.inf, F32))
    top = jnp.max(top, axis=0, keepdims=True) * (SCALE * LOG2E)
    ot[...] = jnp.zeros_like(ot)

    def weigh(b, total):
        at = pl.ds(pl.multiple_of(b * BLOCK, BLOCK), BLOCK)
        w = jnp.exp2(st[at, :] * (SCALE * LOG2E) - top)
        st[at, :] = w
        ot[...] += tn(vs[at, :], w.astype(BF))
        return total + jnp.sum(w.reshape(BLOCK // 8, 8, QROWS), axis=0)

    total = lax.fori_loop(0, steps, weigh, jnp.zeros((8, QROWS), F32))
    inv = 1.0 / jnp.sum(total, axis=0, keepdims=True)
    att = (ot[...] * inv).astype(BF).astype(F32)
    cot_t = cs[...].astype(F32).T
    delta = jnp.sum(att * cot_t, axis=0, keepdims=True)
    att = att.T
    dqt[...] = jnp.zeros_like(dqt)

    for half, ref in ((0, dko_ref), (1, dkx_ref)):
        mine = core if half == 0 else 1 - core

        def back(b, carry):
            at = pl.ds(pl.multiple_of(half * 1024 + b * BLOCK, BLOCK), BLOCK)
            prob = st[at, :] * inv
            dv = nn(prob.astype(BF), cs[...])
            dprod = nt(vs[at, :], cs[...])
            ds = prob * (dprod - delta)
            low_ds = ds.astype(BF)
            dk = nn(low_ds, qe[:, 0:256]) * SCALE
            dqt[...] += tn(ke[at, 0:256], low_ds)
            pooled = jnp.sum(ds.reshape(BLOCK // POOL, POOL, QROWS), axis=1)
            for t in range(BLOCK // 128):
                m = b * (BLOCK // 128) + t
                full, rest = pack_out(dk[t * 128 : (t + 1) * 128])
                ref[m, 0:128, :] = full
                ref[m, 256:320, :] = rest
                full, rest = pack_out(dv[t * 128 : (t + 1) * 128])
                ref[m, 128:256, :] = full
                ref[m, 320:384, :] = rest
                pool[pl.ds(pl.multiple_of(m * 16 + mine * 8, 8), 8), :] = pooled[t * 8 : t * 8 + 8]
            return carry

        lax.fori_loop(0, 1024 // BLOCK, back, 0)

    row = lax.broadcasted_iota(jnp.int32, (QROWS // POOL, QROWS), 0)
    col = lax.broadcasted_iota(jnp.int32, (QROWS // POOL, QROWS), 1)
    pick = jnp.where(row == lax.shift_right_logical(col, 4), 1.0, 0.0).astype(BF)
    hi, lo = split2(pool[...])
    grad_bias = nt(pick, hi) + nt(pick, lo)
    dq = dqt[...].T * SCALE
    for x in range(XS):
        at = slice(x * 128, (x + 1) * 128)
        full, rest = pack_out(att[at])
        oq_ref[x, 0:128, :] = full
        oq_ref[x, 256:320, :] = rest
        full, rest = pack_out(dq[at])
        oq_ref[x, 128:256, :] = full
        oq_ref[x, 320:384, :] = rest
        rows = grad_bias[x * 8 : x * 8 + 8]
        hi = rows.astype(BF).astype(F32)
        oq_ref[x, 384:400, :] = jnp.concatenate([hi, rows - hi], axis=0).astype(BF)


def weight_kernel(oq_ref, pair_ref, out_ref):
    rows = []
    for part in range(2):
        for head in range(HEADS):
            block = oq_ref[head, 384:400, :].astype(F32)[part * 8 : part * 8 + 8]
            rows.append(jnp.concatenate([block[i : i + 1] for i in range(PROW)], axis=1))
    grads = jnp.concatenate(rows, axis=0).astype(BF)
    pair = pair_ref[...].reshape(PROW * PAIRS, 128)
    prod = nn(grads, pair)
    out_ref[...] = prod[0:4] + prod[4:8]


def final_kernel(oq_ref, dkv_ref, wt_ref, att_ref, dq_ref, dk_ref, dv_ref, gp_ref):
    low = low_lanes(64)

    def put(ref, fulls, halves):
        for pair in range(2):
            even, odd = halves[2 * pair], halves[2 * pair + 1]
            mid = jnp.concatenate(
                [jnp.where(low, even, roll_half(odd)), jnp.where(low, roll_half(even), odd)], axis=0
            )
            ref[:, (3 * pair) * 128 : (3 * pair + 1) * 128] = fulls[2 * pair].astype(BF)
            ref[:, (3 * pair + 1) * 128 : (3 * pair + 2) * 128] = mid.astype(BF)
            ref[:, (3 * pair + 2) * 128 : (3 * pair + 3) * 128] = fulls[2 * pair + 1].astype(BF)

    for base, ref in ((0, att_ref), (1, dq_ref)):
        put(
            ref,
            [oq_ref[h, base * 128 : (base + 1) * 128, :] for h in range(HEADS)],
            [oq_ref[h, 256 + base * 64 : 320 + base * 64, :].astype(F32) for h in range(HEADS)],
        )

    def both(h, rows):
        return dkv_ref[h * ZS, rows, :].astype(F32) + dkv_ref[h * ZS + 1, rows, :].astype(F32)

    for base, ref in ((0, dk_ref), (1, dv_ref)):
        put(
            ref,
            [both(h, slice(base * 128, (base + 1) * 128)) for h in range(HEADS)],
            [both(h, slice(256 + base * 64, 320 + base * 64)) for h in range(HEADS)],
        )
    whi, wmid, _ = split3(wt_ref[...])
    blocks = [oq_ref[h, 384:400, :].astype(F32) for h in range(HEADS)]
    wrows = jnp.concatenate([whi.astype(F32), wmid.astype(F32), whi.astype(F32)], axis=0)
    wrows = jnp.concatenate([wrows, jnp.zeros((8, 128), F32)], axis=0).astype(BF)
    zero = jnp.zeros((4, 128), F32)
    for i in range(PROW):
        hi = jnp.concatenate([b[i : i + 1] for b in blocks] + [zero], axis=0)
        lo = jnp.concatenate([b[8 + i : 9 + i] for b in blocks] + [zero], axis=0)
        grads = jnp.concatenate([hi, hi, lo, jnp.zeros((8, 128), F32)], axis=0)
        gp_ref[i] = nn(grads.T.astype(BF), wrows).astype(BF)


def shape(*dims, dtype=BF):
    return jax.ShapeDtypeStruct(dims, dtype)


def call(kernel, out_shape, args, scratch=(), flops=0, moved=0, smem=0, limit=32):
    single = not isinstance(out_shape, tuple)
    return pl.pallas_call(
        kernel,
        out_shape=out_shape,
        in_specs=[SMEM] * smem + [VMEM] * (len(args) - smem),
        out_specs=VMEM if single else (VMEM,) * len(out_shape),
        scratch_shapes=list(scratch),
        cost_estimate=pl.CostEstimate(flops=flops, bytes_accessed=moved, transcendentals=0),
        compiler_params=pltpu.CompilerParams(vmem_limit_bytes=limit * 1024 * 1024),
    )(*args)


def seq_index(x, z, c):
    return (x * ZS + z) * CS + c


def body(dp, queries, keys, values, cotangent, pair, pair_weight):
    x_groups = [[seq_index(x, z, c) for x in range(XS)] for z in range(ZS) for c in range(CS)]
    xz_groups = [[seq_index(x, z, c) for x in range(XS) for z in range(ZS)] for c in range(CS)]
    xc_groups = [[seq_index(x, z, c) for x in range(XS) for c in range(CS)] for z in range(ZS)]
    far_groups = [
        [d * 16 + seq_index(x, z, c) for d in range(dp) for z in range(ZS)]
        for x in range(XS)
        for c in range(CS)
    ]
    swap = [(s, s ^ 1) for s in range(16)]

    def exchange(array, groups, axis="seq"):
        return lax.all_to_all(array, axis, 0, 0, axis_index_groups=groups)

    core = (lax.axis_index("seq") % CS).astype(jnp.int32).reshape(1)
    pair_rows = pair[0]
    wt = jnp.concatenate([pair_weight.T, jnp.zeros((4, 128), F32)], axis=0)
    kv, qd = call(
        pack_kernel,
        (shape(8, 384, 128), shape(4, 400, 128)),
        (queries[0], keys[0], values[0], cotangent[0], pair_rows, wt),
        flops=2 * 24 * 1024 * 128,
        moved=3_000_000,
    )
    kv_own = exchange(kv, xz_groups)
    qd_own = exchange(qd, x_groups)
    kv_other = lax.ppermute(kv_own, "seq", swap)
    oq, dkv_own, dkv_other = call(
        attn_kernel,
        (shape(4, 400, 128), shape(8, 384, 128), shape(8, 384, 128)),
        (core, qd_own, kv_own, kv_other),
        scratch=(
            pltpu.VMEM((KROWS, 512), BF),
            pltpu.VMEM((KROWS, 256), BF),
            pltpu.VMEM((QROWS, 512), BF),
            pltpu.VMEM((QROWS, 256), BF),
            pltpu.VMEM((KROWS, QROWS), F32),
            pltpu.VMEM((256, QROWS), F32),
            pltpu.VMEM((256, QROWS), F32),
            pltpu.VMEM((PAIRS, QROWS), F32),
        ),
        flops=8 * 2 * QROWS * KROWS * 256,
        moved=5_000_000,
        smem=1,
        limit=40,
    )
    dkv_swapped = lax.ppermute(dkv_other, "seq", swap)
    dkv = (dkv_own.astype(F32) + dkv_swapped.astype(F32)).astype(BF)
    dkv_back = exchange(dkv, xz_groups)
    oq_back = exchange(oq, x_groups)
    term = call(
        weight_kernel, shape(4, 128, dtype=F32), (oq_back, pair_rows), flops=2 * 1024 * 128 * 8, moved=300_000
    )
    near = exchange(jnp.broadcast_to(term[None], (8, 4, 128)), xc_groups).sum(axis=0)
    count = dp * ZS
    far = exchange(jnp.broadcast_to(near[None], (count, 4, 128)), far_groups, ("dp", "seq"))
    grad_weight = far.sum(axis=0).T
    att, dq, dk, dv, gp = call(
        final_kernel,
        (shape(128, 768),) * 4 + (shape(PROW, PAIRS, 128),),
        (oq_back, dkv_back, wt),
        flops=2 * 1024 * 128 * 32,
        moved=3_000_000,
    )
    return att[None], dq[None], dk[None], dv[None], gp[None], grad_weight


def solution(mesh):
    rows = P("dp", "seq", None)
    cells = P("dp", "seq", None, None)
    return jax.shard_map(
        functools.partial(body, mesh.shape["dp"]),
        mesh=mesh,
        in_specs=(rows, rows, rows, rows, cells, P()),
        out_specs=(rows, rows, rows, rows, cells, P()),
        check_vma=False,
    )
```

```python
import functools
import math

import jax
import jax.numpy as jnp
from jax import lax
from jax.experimental import pallas as pl
from jax.experimental.pallas import tpu as pltpu
from jax.sharding import PartitionSpec as P

HEADS = 4
HDIM = 192
TOK = 128
POOL = 16
PROW = TOK // POOL
PAIRS = 128
XS = 4
ZS = 2
CS = 2
QROWS = XS * TOK
KROWS = XS * ZS * CS * TOK
BLOCK = 256
SCALE = HDIM ** (-0.5)
LOG2E = 1.0 / math.log(2.0)
BF = jnp.bfloat16
F32 = jnp.float32
VMEM = pl.BlockSpec(memory_space=pltpu.VMEM)
SMEM = pl.BlockSpec(memory_space=pltpu.SMEM)
ANY = pl.BlockSpec(memory_space=pl.ANY)

FULL_TILE = (0, 2, 3, 5)
HALF_TILE = (1, 1, 4, 4)


def nn(a, b):
    return lax.dot_general(a, b, (((1,), (0,)), ((), ())), preferred_element_type=F32)


def nt(a, b):
    return lax.dot_general(a, b, (((1,), (1,)), ((), ())), preferred_element_type=F32)


def tn(a, b):
    return lax.dot_general(a, b, (((0,), (0,)), ((), ())), preferred_element_type=F32)


def roll_half(x):
    return pltpu.roll(x, 64, 1)


def low_lanes(rows):
    return lax.broadcasted_iota(jnp.int32, (rows, 128), 1) < 64


def split2(x):
    hi = x.astype(BF)
    return hi, (x - hi.astype(F32)).astype(BF)


def split3(x):
    hi = x.astype(BF)
    rest = x - hi.astype(F32)
    mid = rest.astype(BF)
    return hi, mid, (rest - mid.astype(F32)).astype(BF)


def pack_heads(ref):
    low = low_lanes(64)
    for pair in range(2):
        tile = ref[:, (3 * pair + 1) * 128 : (3 * pair + 2) * 128].astype(F32)
        top, bottom = tile[:64], tile[64:]
        even = jnp.where(low, top, roll_half(bottom)).astype(BF)
        odd = jnp.where(low, roll_half(top), bottom).astype(BF)
        for parity, half in ((0, even), (1, odd)):
            head = 2 * pair + parity
            full = FULL_TILE[head]
            yield head, ref[:, full * 128 : (full + 1) * 128], half


def pack_kv_kernel(k_hbm, v_hbm, kv_ref, k_vmem, v_vmem, sems):
    copies = [
        pltpu.make_async_copy(k_hbm, k_vmem, sems.at[0]),
        pltpu.make_async_copy(v_hbm, v_vmem, sems.at[1]),
    ]
    for copy in copies:
        copy.start()
    for base, copy, ref in ((0, copies[0], k_vmem), (1, copies[1], v_vmem)):
        copy.wait()
        for head, full, half in pack_heads(ref):
            for zs in range(ZS):
                slot = head * ZS + zs
                kv_ref[slot, base * 128 : (base + 1) * 128, :] = full
                kv_ref[slot, 256 + base * 64 : 320 + base * 64, :] = half


def pack_qd_kernel(
    x_ref, q_hbm, c_hbm, pair_hbm, w_hbm, out0, out1, out2, out3,
    q_vmem, c_vmem, pair_vmem, w_vmem, staged, sems,
):
    copies = [
        pltpu.make_async_copy(q_hbm, q_vmem, sems.at[0]),
        pltpu.make_async_copy(c_hbm, c_vmem, sems.at[1]),
        pltpu.make_async_copy(w_hbm, w_vmem, sems.at[2]),
        pltpu.make_async_copy(pair_hbm, pair_vmem, sems.at[3]),
    ]
    for copy in copies:
        copy.start()
    for base, copy, ref in ((0, copies[0], q_vmem), (1, copies[1], c_vmem)):
        copy.wait()
        for head, full, half in pack_heads(ref):
            staged[head, base * 128 : (base + 1) * 128, :] = full
            staged[head, 256 + base * 64 : 320 + base * 64, :] = half
    copies[2].wait()
    copies[3].wait()
    wt = weight_rows(w_vmem[...])
    parts = jnp.concatenate([p.astype(F32) for p in split3(wt)], axis=0).astype(BF)
    pair = pair_vmem[...].reshape(PROW * PAIRS, 128)
    prod = nt(parts, pair)
    bias = (prod[0:8] + (prod[8:16] + prod[16:24])) * (1.0 / SCALE)
    for head in range(HEADS):
        rows = jnp.concatenate(
            [bias[head : head + 1, i * 128 : (i + 1) * 128] for i in range(PROW)], axis=0
        )
        hi = rows.astype(BF).astype(F32)
        staged[head, 384:400, :] = jnp.concatenate([hi, rows - hi], axis=0).astype(BF)
    x = x_ref[0]
    for k, out in enumerate((out0, out1, out2, out3)):
        out[...] = staged[lax.rem(x + k, XS)]


def weight_rows(weight):
    return jnp.concatenate([weight, jnp.zeros((4, 128), F32)], axis=0)


def unpack(full, half, rows_low):
    half = half.astype(F32)
    top = jnp.where(rows_low, half, 0.0)
    bottom = jnp.where(rows_low, roll_half(half), 0.0)
    other = jnp.concatenate([top, bottom], axis=0).astype(BF)
    return full, other


def pack_out(block):
    rest = block[:, 128:]
    return block[:, :128].astype(BF), (rest[:64] + roll_half(rest[64:])).astype(BF)


def scores_kernel(
    core_ref, qd0, qd1, qd2, qd3, kv_own, kv_other, pb, dsb, ke, qe, cs, att_ref, gb_ref,
    vs, st, ot, pool,
):
    low = low_lanes(64)
    core = core_ref[0]
    for half, kv_ref in enumerate((kv_own, kv_other)):
        mine = core if half == 0 else 1 - core
        for m in range(8):
            base = half * 1024 + m * 128
            full, other = unpack(kv_ref[m, 0:128, :], kv_ref[m, 256:320, :], low)
            ke[base : base + 128, 0:128] = full
            ke[base : base + 128, 128:256] = other
            full, other = unpack(kv_ref[m, 128:256, :], kv_ref[m, 320:384, :], low)
            vs[base : base + 128, 0:128] = full
            vs[base : base + 128, 128:256] = other
        row = lax.broadcasted_iota(jnp.int32, (1024, 128), 0)
        col = lax.broadcasted_iota(jnp.int32, (1024, 128), 1)
        cell = lax.shift_right_logical(row, 7) * 16 + mine * 8 + (lax.shift_right_logical(row, 4) & 7)
        table = jnp.where(cell == col, 1.0, 0.0).astype(BF)
        ke[half * 1024 : (half + 1) * 1024, 256:384] = table
        ke[half * 1024 : (half + 1) * 1024, 384:512] = table
    for k, qd_ref in enumerate((qd0, qd1, qd2, qd3)):
        base = k * 128
        full, other = unpack(qd_ref[0:128, :], qd_ref[256:320, :], low)
        qe[base : base + 128, 0:128] = full
        qe[base : base + 128, 128:256] = other
        full, other = unpack(qd_ref[128:256, :], qd_ref[320:384, :], low)
        cs[base : base + 128, 0:128] = full
        cs[base : base + 128, 128:256] = other
        rows = qd_ref[384:400, :].astype(F32)
        for part in range(2):
            wide = jnp.broadcast_to(rows[part * 8 : part * 8 + 8, None, :], (8, POOL, 128))
            qe[base : base + 128, 256 + part * 128 : 384 + part * 128] = wide.reshape(128, 128).astype(BF)

    steps = KROWS // BLOCK

    def scores(b, top):
        at = pl.ds(pl.multiple_of(b * BLOCK, BLOCK), BLOCK)
        s = nt(ke[at, :], qe[...])
        st[at, :] = s
        return jnp.maximum(top, jnp.max(s.reshape(BLOCK // 8, 8, QROWS), axis=0))

    top = lax.fori_loop(0, steps, scores, jnp.full((8, QROWS), -jnp.inf, F32))
    top = jnp.max(top, axis=0, keepdims=True) * (SCALE * LOG2E)
    ot[...] = jnp.zeros_like(ot)

    def weigh(b, total):
        at = pl.ds(pl.multiple_of(b * BLOCK, BLOCK), BLOCK)
        w = jnp.exp2(st[at, :] * (SCALE * LOG2E) - top)
        st[at, :] = w
        ot[...] += tn(vs[at, :], w.astype(BF))
        return total + jnp.sum(w.reshape(BLOCK // 8, 8, QROWS), axis=0)

    total = lax.fori_loop(0, steps, weigh, jnp.zeros((8, QROWS), F32))
    inv = 1.0 / jnp.sum(total, axis=0, keepdims=True)
    att = (ot[...] * inv).astype(BF).astype(F32)
    delta = jnp.sum(att * cs[...].astype(F32).T, axis=0, keepdims=True)
    att_ref[...] = att.T.astype(BF)

    for half in range(CS):
        mine = core if half == 0 else 1 - core

        def back(b, carry):
            at = pl.ds(pl.multiple_of(half * 1024 + b * BLOCK, BLOCK), BLOCK)
            prob = st[at, :] * inv
            pb[at, :] = prob.astype(BF)
            ds = prob * (nt(vs[at, :], cs[...]) - delta)
            dsb[at, :] = ds.astype(BF)
            pooled = jnp.sum(ds.reshape(BLOCK // POOL, POOL, QROWS), axis=1)
            for t in range(BLOCK // 128):
                m = b * (BLOCK // 128) + t
                pool[pl.ds(pl.multiple_of(m * 16 + mine * 8, 8), 8), :] = pooled[t * 8 : t * 8 + 8]
            return carry

        lax.fori_loop(0, 1024 // BLOCK, back, 0)

    row = lax.broadcasted_iota(jnp.int32, (QROWS // POOL, QROWS), 0)
    col = lax.broadcasted_iota(jnp.int32, (QROWS // POOL, QROWS), 1)
    pick = jnp.where(row == lax.shift_right_logical(col, 4), 1.0, 0.0).astype(BF)
    hi, lo = split2(pool[...])
    grad_bias = nt(pick, hi) + nt(pick, lo)
    gb_ref[...] = grad_bias


def weight_kernel(oq_ref, pair_ref, out_ref):
    rows = []
    for part in range(2):
        for head in range(HEADS):
            block = oq_ref[head, 384:400, :].astype(F32)[part * 8 : part * 8 + 8]
            rows.append(jnp.concatenate([block[i : i + 1] for i in range(PROW)], axis=1))
    prod = nn(jnp.concatenate(rows, axis=0).astype(BF), pair_ref[...].reshape(PROW * PAIRS, 128))
    out_ref[...] = prod[0:4] + prod[4:8]


def grads_kernel(
    x_ref, pb, dsb, ke, qe, cs, att_ref, gb_ref, dko_ref, dkx_ref, oq_ref, dqt
):
    dqt[...] = jnp.zeros_like(dqt)
    for half, ref in ((1, dkx_ref), (0, dko_ref)):

        def back(b, carry):
            at = pl.ds(pl.multiple_of(half * 1024 + b * BLOCK, BLOCK), BLOCK)
            low_ds = dsb[at, :]
            dv = nn(pb[at, :], cs[...])
            dk = nn(low_ds, qe[:, 0:256]) * SCALE
            dqt[...] += tn(ke[at, 0:256], low_ds)
            for t in range(BLOCK // 128):
                m = b * (BLOCK // 128) + t
                full, rest = pack_out(dk[t * 128 : (t + 1) * 128])
                ref[m, 0:128, :] = full
                ref[m, 256:320, :] = rest
                full, rest = pack_out(dv[t * 128 : (t + 1) * 128])
                ref[m, 128:256, :] = full
                ref[m, 320:384, :] = rest
            return carry

        lax.fori_loop(0, 1024 // BLOCK, back, 0)

    dq = dqt[...].T * SCALE
    for k in range(XS):
        to = lax.rem(x_ref[0] + XS - k, XS)
        at = slice(k * 128, (k + 1) * 128)
        full, rest = pack_out(att_ref[at, :].astype(F32))
        oq_ref[to, 0:128, :] = full
        oq_ref[to, 256:320, :] = rest
        full, rest = pack_out(dq[at])
        oq_ref[to, 128:256, :] = full
        oq_ref[to, 320:384, :] = rest
        rows = gb_ref[k * PROW : (k + 1) * PROW, :]
        hi = rows.astype(BF).astype(F32)
        oq_ref[to, 384:400, :] = jnp.concatenate([hi, rows - hi], axis=0).astype(BF)


def cores_kernel(z_ref, own_ref, other_ref, send_ref, keep_ref):
    z = z_ref[0]
    for x in range(XS):
        away = x * ZS + 1 - z
        send_ref[x] = (own_ref[away].astype(F32) + other_ref[away].astype(F32)).astype(BF)
        here = x * ZS + z
        keep_ref[x] = own_ref[here].astype(F32) + other_ref[here].astype(F32)


def merge_kernel(keep_ref, come_ref, far_ref, out_ref):
    total = jnp.sum(far_ref[...], axis=0)
    hi = total.astype(BF).astype(F32)
    rest = total - hi
    mid = rest.astype(BF).astype(F32)
    rows = jnp.concatenate([hi, mid, rest - mid, jnp.zeros((4, 128), F32)], axis=0).astype(BF)
    for x in range(XS):
        out_ref[x, 0:384, :] = (keep_ref[x] + come_ref[x].astype(F32)).astype(BF)
        out_ref[x, 384:400, :] = rows


def put(ref, fulls, halves):
    low = low_lanes(64)
    for pair in range(2):
        even, odd = halves[2 * pair], halves[2 * pair + 1]
        mid = jnp.concatenate(
            [jnp.where(low, even, roll_half(odd)), jnp.where(low, roll_half(even), odd)], axis=0
        )
        ref[:, (3 * pair) * 128 : (3 * pair + 1) * 128] = fulls[2 * pair].astype(BF)
        ref[:, (3 * pair + 1) * 128 : (3 * pair + 2) * 128] = mid.astype(BF)
        ref[:, (3 * pair + 2) * 128 : (3 * pair + 3) * 128] = fulls[2 * pair + 1].astype(BF)


def query_kernel(oq_ref, w_ref, att_ref, dq_ref, gp_ref):
    for base, ref in ((0, att_ref), (1, dq_ref)):
        put(
            ref,
            [oq_ref[h, base * 128 : (base + 1) * 128, :] for h in range(HEADS)],
            [oq_ref[h, 256 + base * 64 : 320 + base * 64, :].astype(F32) for h in range(HEADS)],
        )
    whi, wmid, _ = split3(w_ref[...])
    wrows = jnp.concatenate([whi.astype(F32), wmid.astype(F32), whi.astype(F32)], axis=0)
    wrows = jnp.concatenate([wrows, jnp.zeros((4, 128), F32)], axis=0).astype(BF)
    blocks = [oq_ref[h, 384:400, :].astype(F32) for h in range(HEADS)]
    zero = jnp.zeros((4, 128), F32)
    for i in range(PROW):
        hi = jnp.concatenate([b[i : i + 1] for b in blocks], axis=0)
        lo = jnp.concatenate([b[8 + i : 9 + i] for b in blocks], axis=0)
        grads = jnp.concatenate([hi, hi, lo, zero], axis=0)
        gp_ref[i] = nn(grads.T.astype(BF), wrows).astype(BF)


def key_kernel(dkv_ref, dk_ref, dv_ref, gw_ref):
    for base, ref in ((0, dk_ref), (1, dv_ref)):
        put(
            ref,
            [dkv_ref[h, base * 128 : (base + 1) * 128, :] for h in range(HEADS)],
            [dkv_ref[h, 256 + base * 64 : 320 + base * 64, :].astype(F32) for h in range(HEADS)],
        )
    total = jnp.zeros((16, 128), F32)
    for x in range(XS):
        total += dkv_ref[x, 384:400, :].astype(F32)
    gw_ref[...] = (total[8:12] + total[4:8]) + total[0:4]


def shape(*dims, dtype=BF):
    return jax.ShapeDtypeStruct(dims, dtype)


def call(kernel, out_shape, args, scratch=(), flops=0, moved=0, smem=0, hbm=0, limit=32):
    single = not isinstance(out_shape, tuple)
    rest = len(args) - smem - hbm
    return pl.pallas_call(
        kernel,
        out_shape=out_shape,
        in_specs=[SMEM] * smem + [ANY] * hbm + [VMEM] * rest,
        out_specs=VMEM if single else (VMEM,) * len(out_shape),
        scratch_shapes=list(scratch),
        cost_estimate=pl.CostEstimate(flops=flops, bytes_accessed=moved, transcendentals=0),
        compiler_params=pltpu.CompilerParams(vmem_limit_bytes=limit * 1024 * 1024),
    )(*args)


def seq_index(x, z, c):
    return (x * ZS + z) * CS + c


def body(dp, queries, keys, values, cotangent, pair, pair_weight):
    xz_groups = [[seq_index(x, z, c) for x in range(XS) for z in range(ZS)] for c in range(CS)]
    x_groups = [[seq_index(x, z, c) for x in range(XS)] for z in range(ZS) for c in range(CS)]
    far_groups = [
        [d * 16 + seq_index(x, z, c) for d in range(dp) for z in range(ZS)]
        for x in range(XS)
        for c in range(CS)
    ]
    across = [
        (seq_index(x, z, c), seq_index(x, 1 - z, c))
        for x in range(XS)
        for z in range(ZS)
        for c in range(CS)
    ]
    swap = [(s, s ^ 1) for s in range(16)]

    def ring(k):
        return [
            (seq_index(x, z, c), seq_index((x + k) % XS, z, c))
            for x in range(XS)
            for z in range(ZS)
            for c in range(CS)
        ]

    place = lax.axis_index("seq").astype(jnp.int32)
    core = (place % CS).reshape(1)
    own_z = (place // CS % ZS).reshape(1)
    own_x = (place // (ZS * CS)).reshape(1)
    pair_rows = pair[0]
    kv = call(
        pack_kv_kernel,
        shape(8, 384, 128),
        (keys[0], values[0]),
        hbm=2,
        scratch=(pltpu.VMEM((TOK, 768), BF), pltpu.VMEM((TOK, 768), BF), pltpu.SemaphoreType.DMA((2,))),
        moved=1_500_000,
        limit=56,
    )
    kv, query_rows, cot_rows = lax.optimization_barrier((kv, queries[0], cotangent[0]))
    kv_own = lax.all_to_all(kv, "seq", 0, 0, axis_index_groups=xz_groups)
    qd = call(
        pack_qd_kernel,
        (shape(400, 128),) * XS,
        (own_x, query_rows, cot_rows, pair_rows, pair_weight.T),
        smem=1,
        hbm=4,
        scratch=(
            pltpu.VMEM((TOK, 768), BF),
            pltpu.VMEM((TOK, 768), BF),
            pltpu.VMEM((PROW, PAIRS, 128), BF),
            pltpu.VMEM((HEADS, 128), F32),
            pltpu.VMEM((HEADS, 400, 128), BF),
            pltpu.SemaphoreType.DMA((4,)),
        ),
        flops=2 * 24 * 1024 * 128,
        moved=1_500_000,
        limit=8,
    )
    qd = [qd[0]] + [lax.ppermute(qd[k], "seq", ring(k)) for k in range(1, XS)]
    kv_own, qd = lax.optimization_barrier((kv_own, qd))
    kv_other = lax.ppermute(kv_own, "seq", swap)
    pb, dsb, ke, qe, cs, att, gb = call(
        scores_kernel,
        (
            shape(KROWS, QROWS), shape(KROWS, QROWS), shape(KROWS, 512), shape(QROWS, 512),
            shape(QROWS, 256), shape(QROWS, 256), shape(XS * PROW, 128, dtype=F32),
        ),
        (core, *qd, kv_own, kv_other),
        smem=1,
        scratch=(
            pltpu.VMEM((KROWS, 256), BF),
            pltpu.VMEM((KROWS, QROWS), F32),
            pltpu.VMEM((256, QROWS), F32),
            pltpu.VMEM((PAIRS, QROWS), F32),
        ),
        flops=4 * 2 * QROWS * KROWS * 256,
        moved=8_000_000,
        limit=32,
    )
    count = dp * ZS
    dkv_own, dkv_other, oq = call(
        grads_kernel,
        (shape(8, 384, 128), shape(8, 384, 128), shape(XS, 400, 128)),
        (own_x, pb, dsb, ke, qe, cs, att, gb),
        smem=1,
        scratch=(pltpu.VMEM((256, QROWS), F32),),
        flops=3 * 2 * QROWS * KROWS * 256,
        moved=8_000_000,
        limit=16,
    )
    oq = lax.all_to_all(oq, "seq", 0, 0, axis_index_groups=x_groups)
    dkv_swapped = lax.ppermute(dkv_other, "seq", swap)
    send, keep = call(
        cores_kernel,
        (shape(XS, 384, 128), shape(XS, 384, 128, dtype=F32)),
        (own_z, dkv_own, dkv_swapped),
        smem=1,
        moved=2_400_000,
        limit=8,
    )
    send, oq = lax.optimization_barrier((send, oq))
    come = lax.ppermute(send, "seq", across)
    term = call(
        weight_kernel, shape(HEADS, 128, dtype=F32), (oq, pair_rows),
        flops=2 * 1024 * 128 * 8, moved=500_000, limit=8,
    )
    term = term + lax.ppermute(term, "seq", swap)
    spread = jnp.broadcast_to(term[None], (count, HEADS, 128))
    far = lax.all_to_all(spread, ("dp", "seq"), 0, 0, axis_index_groups=far_groups)
    att, dq, gp = call(
        query_kernel,
        (shape(128, 768), shape(128, 768), shape(PROW, PAIRS, 128)),
        (oq, pair_weight.T),
        flops=2 * 1024 * 128 * 16,
        moved=1_100_000,
        limit=8,
    )
    dkv = call(
        merge_kernel, shape(XS, 400, 128), (keep, come, far), moved=1_600_000, limit=8
    )
    dkv_back = lax.all_to_all(dkv, "seq", 0, 0, axis_index_groups=x_groups)
    dk, dv, gw = call(
        key_kernel,
        (shape(128, 768), shape(128, 768), shape(HEADS, 128, dtype=F32)),
        (dkv_back,),
        moved=800_000,
        limit=8,
    )
    return att[None], dq[None], dk[None], dv[None], gp[None], gw.T


def solution(mesh):
    rows = P("dp", "seq", None)
    cells = P("dp", "seq", None, None)
    return jax.shard_map(
        functools.partial(body, mesh.shape["dp"]),
        mesh=mesh,
        in_specs=(rows, rows, rows, rows, cells, P()),
        out_specs=(rows, rows, rows, rows, cells, P()),
        check_vma=False,
    )
```

```python
import functools
import math

import jax
import jax.numpy as jnp
from jax import lax
from jax.experimental import pallas as pl
from jax.experimental.pallas import tpu as pltpu
from jax.sharding import PartitionSpec as P

HEADS = 4
HDIM = 192
TOK = 128
POOL = 16
PROW = TOK // POOL
PAIRS = 128
XS = 4
ZS = 2
CS = 2
QROWS = XS * TOK
KROWS = XS * ZS * CS * TOK
BLOCK = 1024
UNROLL = 2
SCALE = HDIM ** (-0.5)
LOG2E = 1.0 / math.log(2.0)
BF = jnp.bfloat16
F32 = jnp.float32
VMEM = pl.BlockSpec(memory_space=pltpu.VMEM)
SMEM = pl.BlockSpec(memory_space=pltpu.SMEM)
ANY = pl.BlockSpec(memory_space=pl.ANY)

FULL_TILE = (0, 2, 3, 5)
HALF_TILE = (1, 1, 4, 4)


def nn(a, b):
    return lax.dot_general(a, b, (((1,), (0,)), ((), ())), preferred_element_type=F32)


def nt(a, b):
    return lax.dot_general(a, b, (((1,), (1,)), ((), ())), preferred_element_type=F32)


def tn(a, b):
    return lax.dot_general(a, b, (((0,), (0,)), ((), ())), preferred_element_type=F32)


def roll_half(x):
    return pltpu.roll(x, 64, 1)


def low_lanes(rows):
    return lax.broadcasted_iota(jnp.int32, (rows, 128), 1) < 64


def split2(x):
    hi = x.astype(BF)
    return hi, (x - hi.astype(F32)).astype(BF)


def split3(x):
    hi = x.astype(BF)
    rest = x - hi.astype(F32)
    mid = rest.astype(BF)
    return hi, mid, (rest - mid.astype(F32)).astype(BF)


def pack_heads(ref):
    low = low_lanes(64)
    for pair in range(2):
        tile = ref[:, (3 * pair + 1) * 128 : (3 * pair + 2) * 128].astype(F32)
        top, bottom = tile[:64], tile[64:]
        even = jnp.where(low, top, roll_half(bottom)).astype(BF)
        odd = jnp.where(low, roll_half(top), bottom).astype(BF)
        for parity, half in ((0, even), (1, odd)):
            head = 2 * pair + parity
            full = FULL_TILE[head]
            yield head, ref[:, full * 128 : (full + 1) * 128], half


def pack_kv_kernel(k_hbm, v_hbm, kv_ref, k_vmem, v_vmem, sems):
    copies = [
        pltpu.make_async_copy(k_hbm, k_vmem, sems.at[0]),
        pltpu.make_async_copy(v_hbm, v_vmem, sems.at[1]),
    ]
    for copy in copies:
        copy.start()
    for base, copy, ref in ((0, copies[0], k_vmem), (1, copies[1], v_vmem)):
        copy.wait()
        for head, full, half in pack_heads(ref):
            for zs in range(ZS):
                slot = head * ZS + zs
                kv_ref[slot, base * 128 : (base + 1) * 128, :] = full
                kv_ref[slot, 256 + base * 64 : 320 + base * 64, :] = half


def pack_qd_kernel(
    x_ref, q_hbm, c_hbm, pair_hbm, w_hbm, out0, out1, out2, out3,
    q_vmem, c_vmem, pair_vmem, w_vmem, staged, sems,
):
    copies = [
        pltpu.make_async_copy(q_hbm, q_vmem, sems.at[0]),
        pltpu.make_async_copy(c_hbm, c_vmem, sems.at[1]),
        pltpu.make_async_copy(w_hbm, w_vmem, sems.at[2]),
        pltpu.make_async_copy(pair_hbm, pair_vmem, sems.at[3]),
    ]
    for copy in copies:
        copy.start()
    for base, copy, ref in ((0, copies[0], q_vmem), (1, copies[1], c_vmem)):
        copy.wait()
        for head, full, half in pack_heads(ref):
            staged[head, base * 128 : (base + 1) * 128, :] = full
            staged[head, 256 + base * 64 : 320 + base * 64, :] = half
    copies[2].wait()
    copies[3].wait()
    wt = weight_rows(w_vmem[...])
    parts = jnp.concatenate([p.astype(F32) for p in split3(wt)], axis=0).astype(BF)
    pair = pair_vmem[...].reshape(PROW * PAIRS, 128)
    prod = nt(parts, pair)
    bias = (prod[0:8] + (prod[8:16] + prod[16:24])) * (1.0 / SCALE)
    for head in range(HEADS):
        rows = jnp.concatenate(
            [bias[head : head + 1, i * 128 : (i + 1) * 128] for i in range(PROW)], axis=0
        )
        hi = rows.astype(BF).astype(F32)
        staged[head, 384:400, :] = jnp.concatenate([hi, rows - hi], axis=0).astype(BF)
    x = x_ref[0]
    for k, out in enumerate((out0, out1, out2, out3)):
        out[...] = staged[lax.rem(x + k, XS)]


def weight_rows(weight):
    return jnp.concatenate([weight, jnp.zeros((4, 128), F32)], axis=0)


def unpack(full, half, rows_low):
    half = half.astype(F32)
    top = jnp.where(rows_low, half, 0.0)
    bottom = jnp.where(rows_low, roll_half(half), 0.0)
    other = jnp.concatenate([top, bottom], axis=0).astype(BF)
    return full, other


def pack_out(block):
    rest = block[:, 128:]
    return block[:, :128].astype(BF), (rest[:64] + roll_half(rest[64:])).astype(BF)


def loop(steps, body, init):
    return lax.fori_loop(0, steps, body, init, unroll=UNROLL)


def attn_kernel(
    core_ref, x_ref, kv_other, qd0, qd1, qd2, qd3, kv_own, dko_ref, dkx_ref, oq_ref,
    ke, vs, qe, cs, st, ot, dqt, pool, kv_vmem, sem,
):
    low = low_lanes(64)
    core = core_ref[0]
    fetch = pltpu.make_async_copy(kv_other, kv_vmem, sem)
    fetch.start()
    for half, kv_ref in enumerate((kv_own, kv_vmem)):
        if half == 1:
            fetch.wait()
        mine = core if half == 0 else 1 - core
        for m in range(8):
            base = half * 1024 + m * 128
            full, other = unpack(kv_ref[m, 0:128, :], kv_ref[m, 256:320, :], low)
            ke[base : base + 128, 0:128] = full
            ke[base : base + 128, 128:256] = other
            full, other = unpack(kv_ref[m, 128:256, :], kv_ref[m, 320:384, :], low)
            vs[base : base + 128, 0:128] = full
            vs[base : base + 128, 128:256] = other
        row = lax.broadcasted_iota(jnp.int32, (1024, 128), 0)
        col = lax.broadcasted_iota(jnp.int32, (1024, 128), 1)
        cell = lax.shift_right_logical(row, 7) * 16 + mine * 8 + (lax.shift_right_logical(row, 4) & 7)
        table = jnp.where(cell == col, 1.0, 0.0).astype(BF)
        ke[half * 1024 : (half + 1) * 1024, 256:384] = table
        ke[half * 1024 : (half + 1) * 1024, 384:512] = table
    for k, qd_ref in enumerate((qd0, qd1, qd2, qd3)):
        base = k * 128
        full, other = unpack(qd_ref[0:128, :], qd_ref[256:320, :], low)
        qe[base : base + 128, 0:128] = full
        qe[base : base + 128, 128:256] = other
        full, other = unpack(qd_ref[128:256, :], qd_ref[320:384, :], low)
        cs[base : base + 128, 0:128] = full
        cs[base : base + 128, 128:256] = other
        rows = qd_ref[384:400, :].astype(F32)
        for part in range(2):
            wide = jnp.broadcast_to(rows[part * 8 : part * 8 + 8, None, :], (8, POOL, 128))
            qe[base : base + 128, 256 + part * 128 : 384 + part * 128] = wide.reshape(128, 128).astype(BF)

    steps = KROWS // BLOCK

    def scores(b, top):
        at = pl.ds(pl.multiple_of(b * BLOCK, BLOCK), BLOCK)
        s = nt(ke[at, :], qe[...])
        st[at, :] = s
        return jnp.maximum(top, jnp.max(s.reshape(BLOCK // 8, 8, QROWS), axis=0))

    top = loop(steps, scores, jnp.full((8, QROWS), -jnp.inf, F32))
    top = jnp.max(top, axis=0, keepdims=True) * (SCALE * LOG2E)
    ot[...] = jnp.zeros_like(ot)

    def weigh(b, total):
        at = pl.ds(pl.multiple_of(b * BLOCK, BLOCK), BLOCK)
        w = jnp.exp2(st[at, :] * (SCALE * LOG2E) - top)
        st[at, :] = w
        ot[...] += tn(vs[at, :], w.astype(BF))
        return total + jnp.sum(w.reshape(BLOCK // 8, 8, QROWS), axis=0)

    total = loop(steps, weigh, jnp.zeros((8, QROWS), F32))
    inv = 1.0 / jnp.sum(total, axis=0, keepdims=True)
    att = (ot[...] * inv).astype(BF).astype(F32)
    delta = jnp.sum(att * cs[...].astype(F32).T, axis=0, keepdims=True)
    att = att.T
    dqt[...] = jnp.zeros_like(dqt)

    for half, ref in ((0, dko_ref), (1, dkx_ref)):
        mine = core if half == 0 else 1 - core

        def back(b, carry):
            at = pl.ds(pl.multiple_of(half * 1024 + b * BLOCK, BLOCK), BLOCK)
            prob = st[at, :] * inv
            dv = nn(prob.astype(BF), cs[...])
            ds = prob * (nt(vs[at, :], cs[...]) - delta)
            low_ds = ds.astype(BF)
            dk = nn(low_ds, qe[:, 0:256]) * SCALE
            dqt[...] += tn(ke[at, 0:256], low_ds)
            pooled = jnp.sum(ds.reshape(BLOCK // POOL, POOL, QROWS), axis=1)
            for t in range(BLOCK // 128):
                m = b * (BLOCK // 128) + t
                full, rest = pack_out(dk[t * 128 : (t + 1) * 128])
                ref[m, 0:128, :] = full
                ref[m, 256:320, :] = rest
                full, rest = pack_out(dv[t * 128 : (t + 1) * 128])
                ref[m, 128:256, :] = full
                ref[m, 320:384, :] = rest
                pool[pl.ds(pl.multiple_of(m * 16 + mine * 8, 8), 8), :] = pooled[t * 8 : t * 8 + 8]
            return carry

        loop(1024 // BLOCK, back, 0)

    row = lax.broadcasted_iota(jnp.int32, (QROWS // POOL, QROWS), 0)
    col = lax.broadcasted_iota(jnp.int32, (QROWS // POOL, QROWS), 1)
    pick = jnp.where(row == lax.shift_right_logical(col, 4), 1.0, 0.0).astype(BF)
    hi, lo = split2(pool[...])
    grad_bias = nt(pick, hi) + nt(pick, lo)
    dq = dqt[...].T * SCALE
    for k in range(XS):
        to = lax.rem(x_ref[0] + XS - k, XS)
        at = slice(k * 128, (k + 1) * 128)
        full, rest = pack_out(att[at])
        oq_ref[to, 0:128, :] = full
        oq_ref[to, 256:320, :] = rest
        full, rest = pack_out(dq[at])
        oq_ref[to, 128:256, :] = full
        oq_ref[to, 320:384, :] = rest
        rows = grad_bias[k * PROW : (k + 1) * PROW]
        hi = rows.astype(BF).astype(F32)
        oq_ref[to, 384:400, :] = jnp.concatenate([hi, rows - hi], axis=0).astype(BF)


def weight_kernel(oq_ref, pair_ref, out_ref):
    rows = []
    for part in range(2):
        for head in range(HEADS):
            block = oq_ref[head, 384:400, :].astype(F32)[part * 8 : part * 8 + 8]
            rows.append(jnp.concatenate([block[i : i + 1] for i in range(PROW)], axis=1))
    prod = nn(jnp.concatenate(rows, axis=0).astype(BF), pair_ref[...].reshape(PROW * PAIRS, 128))
    out_ref[...] = prod[0:4] + prod[4:8]


def grads_kernel(
    x_ref, pb, dsb, ke, qe, cs, att_ref, gb_ref, dko_ref, dkx_ref, oq_ref, dqt
):
    dqt[...] = jnp.zeros_like(dqt)
    for half, ref in ((1, dkx_ref), (0, dko_ref)):

        def back(b, carry):
            at = pl.ds(pl.multiple_of(half * 1024 + b * BLOCK, BLOCK), BLOCK)
            low_ds = dsb[at, :]
            dv = nn(pb[at, :], cs[...])
            dk = nn(low_ds, qe[:, 0:256]) * SCALE
            dqt[...] += tn(ke[at, 0:256], low_ds)
            for t in range(BLOCK // 128):
                m = b * (BLOCK // 128) + t
                full, rest = pack_out(dk[t * 128 : (t + 1) * 128])
                ref[m, 0:128, :] = full
                ref[m, 256:320, :] = rest
                full, rest = pack_out(dv[t * 128 : (t + 1) * 128])
                ref[m, 128:256, :] = full
                ref[m, 320:384, :] = rest
            return carry

        lax.fori_loop(0, 1024 // BLOCK, back, 0)

    dq = dqt[...].T * SCALE
    for k in range(XS):
        to = lax.rem(x_ref[0] + XS - k, XS)
        at = slice(k * 128, (k + 1) * 128)
        full, rest = pack_out(att_ref[at, :].astype(F32))
        oq_ref[to, 0:128, :] = full
        oq_ref[to, 256:320, :] = rest
        full, rest = pack_out(dq[at])
        oq_ref[to, 128:256, :] = full
        oq_ref[to, 320:384, :] = rest
        rows = gb_ref[k * PROW : (k + 1) * PROW, :]
        hi = rows.astype(BF).astype(F32)
        oq_ref[to, 384:400, :] = jnp.concatenate([hi, rows - hi], axis=0).astype(BF)


def cores_kernel(z_ref, own_ref, other_ref, send_ref, keep_ref):
    z = z_ref[0]
    for x in range(XS):
        away = x * ZS + 1 - z
        send_ref[x] = (own_ref[away].astype(F32) + other_ref[away].astype(F32)).astype(BF)
        here = x * ZS + z
        keep_ref[x] = own_ref[here].astype(F32) + other_ref[here].astype(F32)


def merge_kernel(keep_ref, come_ref, far_ref, out_ref):
    total = jnp.sum(far_ref[...], axis=0)
    hi = total.astype(BF).astype(F32)
    rest = total - hi
    mid = rest.astype(BF).astype(F32)
    rows = jnp.concatenate([hi, mid, rest - mid, jnp.zeros((4, 128), F32)], axis=0).astype(BF)
    for x in range(XS):
        out_ref[x, 0:384, :] = (keep_ref[x] + come_ref[x].astype(F32)).astype(BF)
        out_ref[x, 384:400, :] = rows


def put(ref, fulls, halves):
    low = low_lanes(64)
    for pair in range(2):
        even, odd = halves[2 * pair], halves[2 * pair + 1]
        mid = jnp.concatenate(
            [jnp.where(low, even, roll_half(odd)), jnp.where(low, roll_half(even), odd)], axis=0
        )
        ref[:, (3 * pair) * 128 : (3 * pair + 1) * 128] = fulls[2 * pair].astype(BF)
        ref[:, (3 * pair + 1) * 128 : (3 * pair + 2) * 128] = mid.astype(BF)
        ref[:, (3 * pair + 2) * 128 : (3 * pair + 3) * 128] = fulls[2 * pair + 1].astype(BF)


def query_kernel(oq_ref, w_ref, att_ref, dq_ref, gp_ref):
    for base, ref in ((0, att_ref), (1, dq_ref)):
        put(
            ref,
            [oq_ref[h, base * 128 : (base + 1) * 128, :] for h in range(HEADS)],
            [oq_ref[h, 256 + base * 64 : 320 + base * 64, :].astype(F32) for h in range(HEADS)],
        )
    whi, wmid, _ = split3(w_ref[...])
    wrows = jnp.concatenate([whi.astype(F32), wmid.astype(F32), whi.astype(F32)], axis=0)
    wrows = jnp.concatenate([wrows, jnp.zeros((4, 128), F32)], axis=0).astype(BF)
    blocks = [oq_ref[h, 384:400, :].astype(F32) for h in range(HEADS)]
    zero = jnp.zeros((4, 128), F32)
    for i in range(PROW):
        hi = jnp.concatenate([b[i : i + 1] for b in blocks], axis=0)
        lo = jnp.concatenate([b[8 + i : 9 + i] for b in blocks], axis=0)
        grads = jnp.concatenate([hi, hi, lo, zero], axis=0)
        gp_ref[i] = nn(grads.T.astype(BF), wrows).astype(BF)


def key_kernel(dkv_ref, dk_ref, dv_ref, gw_ref):
    for base, ref in ((0, dk_ref), (1, dv_ref)):
        put(
            ref,
            [dkv_ref[h, base * 128 : (base + 1) * 128, :] for h in range(HEADS)],
            [dkv_ref[h, 256 + base * 64 : 320 + base * 64, :].astype(F32) for h in range(HEADS)],
        )
    total = jnp.zeros((16, 128), F32)
    for x in range(XS):
        total += dkv_ref[x, 384:400, :].astype(F32)
    gw_ref[...] = (total[8:12] + total[4:8]) + total[0:4]


def shape(*dims, dtype=BF):
    return jax.ShapeDtypeStruct(dims, dtype)


def call(kernel, out_shape, args, scratch=(), flops=0, moved=0, smem=0, hbm=0, limit=32):
    single = not isinstance(out_shape, tuple)
    rest = len(args) - smem - hbm
    return pl.pallas_call(
        kernel,
        out_shape=out_shape,
        in_specs=[SMEM] * smem + [ANY] * hbm + [VMEM] * rest,
        out_specs=VMEM if single else (VMEM,) * len(out_shape),
        scratch_shapes=list(scratch),
        cost_estimate=pl.CostEstimate(flops=flops, bytes_accessed=moved, transcendentals=0),
        compiler_params=pltpu.CompilerParams(vmem_limit_bytes=limit * 1024 * 1024),
    )(*args)


def attention(*args):
    return call(
        attn_kernel,
        (shape(8, 384, 128), shape(8, 384, 128), shape(XS, 400, 128)),
        args,
        smem=2,
        hbm=1,
        scratch=(
            pltpu.VMEM((KROWS, 512), BF),
            pltpu.VMEM((KROWS, 256), BF),
            pltpu.VMEM((QROWS, 512), BF),
            pltpu.VMEM((QROWS, 256), BF),
            pltpu.VMEM((KROWS, QROWS), F32),
            pltpu.VMEM((256, QROWS), F32),
            pltpu.VMEM((256, QROWS), F32),
            pltpu.VMEM((PAIRS, QROWS), F32),
            pltpu.VMEM((8, 384, 128), BF),
            pltpu.SemaphoreType.DMA(()),
        ),
        flops=8 * 2 * QROWS * KROWS * 256,
        moved=5_000_000,
        limit=32,
    )


def seq_index(x, z, c):
    return (x * ZS + z) * CS + c


def body(dp, queries, keys, values, cotangent, pair, pair_weight):
    xz_groups = [[seq_index(x, z, c) for x in range(XS) for z in range(ZS)] for c in range(CS)]
    x_groups = [[seq_index(x, z, c) for x in range(XS)] for z in range(ZS) for c in range(CS)]
    far_groups = [
        [d * 16 + seq_index(x, z, c) for d in range(dp) for z in range(ZS)]
        for x in range(XS)
        for c in range(CS)
    ]
    across = [
        (seq_index(x, z, c), seq_index(x, 1 - z, c))
        for x in range(XS)
        for z in range(ZS)
        for c in range(CS)
    ]
    swap = [(s, s ^ 1) for s in range(16)]

    def ring(k):
        return [
            (seq_index(x, z, c), seq_index((x + k) % XS, z, c))
            for x in range(XS)
            for z in range(ZS)
            for c in range(CS)
        ]

    place = lax.axis_index("seq").astype(jnp.int32)
    core = (place % CS).reshape(1)
    own_z = (place // CS % ZS).reshape(1)
    own_x = (place // (ZS * CS)).reshape(1)
    pair_rows = pair[0]
    kv = call(
        pack_kv_kernel,
        shape(8, 384, 128),
        (keys[0], values[0]),
        hbm=2,
        scratch=(pltpu.VMEM((TOK, 768), BF), pltpu.VMEM((TOK, 768), BF), pltpu.SemaphoreType.DMA((2,))),
        moved=1_500_000,
        limit=56,
    )
    kv, query_rows, cot_rows = lax.optimization_barrier((kv, queries[0], cotangent[0]))
    kv_own = lax.all_to_all(kv, "seq", 0, 0, axis_index_groups=xz_groups)
    qd = call(
        pack_qd_kernel,
        (shape(400, 128),) * XS,
        (own_x, query_rows, cot_rows, pair_rows, pair_weight.T),
        smem=1,
        hbm=4,
        scratch=(
            pltpu.VMEM((TOK, 768), BF),
            pltpu.VMEM((TOK, 768), BF),
            pltpu.VMEM((PROW, PAIRS, 128), BF),
            pltpu.VMEM((HEADS, 128), F32),
            pltpu.VMEM((HEADS, 400, 128), BF),
            pltpu.SemaphoreType.DMA((4,)),
        ),
        flops=2 * 24 * 1024 * 128,
        moved=1_500_000,
        limit=8,
    )
    qd = [qd[0]] + [lax.ppermute(qd[k], "seq", ring(k)) for k in range(1, XS)]
    kv_own, qd = lax.optimization_barrier((kv_own, qd))
    kv_other = lax.ppermute(kv_own, "seq", swap)
    kv_other = pltpu.with_memory_space_constraint(kv_other, pltpu.MemorySpace.HBM)
    count = dp * ZS
    dkv_own, dkv_other, oq = attention(core, own_x, kv_other, *qd, kv_own)
    oq = lax.all_to_all(oq, "seq", 0, 0, axis_index_groups=x_groups)
    dkv_swapped = lax.ppermute(dkv_other, "seq", swap)
    send, keep = call(
        cores_kernel,
        (shape(XS, 384, 128), shape(XS, 384, 128, dtype=F32)),
        (own_z, dkv_own, dkv_swapped),
        smem=1,
        moved=2_400_000,
        limit=8,
    )
    come = lax.ppermute(send, "seq", across)
    term = call(
        weight_kernel, shape(HEADS, 128, dtype=F32), (oq, pair_rows),
        flops=2 * 1024 * 128 * 8, moved=500_000, limit=8,
    )
    term = term + lax.ppermute(term, "seq", swap)
    spread = jnp.broadcast_to(term[None], (count, HEADS, 128))
    far = lax.all_to_all(spread, ("dp", "seq"), 0, 0, axis_index_groups=far_groups)
    att, dq, gp = call(
        query_kernel,
        (shape(128, 768), shape(128, 768), shape(PROW, PAIRS, 128)),
        (oq, pair_weight.T),
        flops=2 * 1024 * 128 * 16,
        moved=1_100_000,
        limit=8,
    )
    dkv = call(
        merge_kernel, shape(XS, 400, 128), (keep, come, far), moved=1_600_000, limit=8
    )
    dkv_back = lax.all_to_all(dkv, "seq", 0, 0, axis_index_groups=x_groups)
    dk, dv, gw = call(
        key_kernel,
        (shape(128, 768), shape(128, 768), shape(HEADS, 128, dtype=F32)),
        (dkv_back,),
        moved=800_000,
        limit=8,
    )
    return att[None], dq[None], dk[None], dv[None], gp[None], gw.T


def solution(mesh):
    rows = P("dp", "seq", None)
    cells = P("dp", "seq", None, None)
    return jax.shard_map(
        functools.partial(body, mesh.shape["dp"]),
        mesh=mesh,
        in_specs=(rows, rows, rows, rows, cells, P()),
        out_specs=(rows, rows, rows, rows, cells, P()),
        check_vma=False,
    )
```

```python
import functools
import math

import jax
import jax.numpy as jnp
from jax import lax
from jax.experimental import pallas as pl
from jax.experimental.pallas import tpu as pltpu
from jax.sharding import PartitionSpec as P

HEADS = 4
HDIM = 192
TOK = 128
POOL = 16
PROW = TOK // POOL
PAIRS = 128
XS = 4
ZS = 2
CS = 2
QROWS = XS * TOK
KROWS = XS * ZS * CS * TOK
BLOCK = 1024
UNROLL = 2
SCALE = HDIM ** (-0.5)
LOG2E = 1.0 / math.log(2.0)
BF = jnp.bfloat16
F32 = jnp.float32
VMEM = pl.BlockSpec(memory_space=pltpu.VMEM)
SMEM = pl.BlockSpec(memory_space=pltpu.SMEM)
ANY = pl.BlockSpec(memory_space=pl.ANY)

FULL_TILE = (0, 2, 3, 5)
HALF_TILE = (1, 1, 4, 4)


def nn(a, b):
    return lax.dot_general(a, b, (((1,), (0,)), ((), ())), preferred_element_type=F32)


def nt(a, b):
    return lax.dot_general(a, b, (((1,), (1,)), ((), ())), preferred_element_type=F32)


def tn(a, b):
    return lax.dot_general(a, b, (((0,), (0,)), ((), ())), preferred_element_type=F32)


def roll_half(x):
    return pltpu.roll(x, 64, 1)


def low_lanes(rows):
    return lax.broadcasted_iota(jnp.int32, (rows, 128), 1) < 64


def split2(x):
    hi = x.astype(BF)
    return hi, (x - hi.astype(F32)).astype(BF)


def split3(x):
    hi = x.astype(BF)
    rest = x - hi.astype(F32)
    mid = rest.astype(BF)
    return hi, mid, (rest - mid.astype(F32)).astype(BF)


def pack_heads(ref):
    low = low_lanes(64)
    for pair in range(2):
        tile = ref[:, (3 * pair + 1) * 128 : (3 * pair + 2) * 128].astype(F32)
        top, bottom = tile[:64], tile[64:]
        even = jnp.where(low, top, roll_half(bottom)).astype(BF)
        odd = jnp.where(low, roll_half(top), bottom).astype(BF)
        for parity, half in ((0, even), (1, odd)):
            head = 2 * pair + parity
            full = FULL_TILE[head]
            yield head, ref[:, full * 128 : (full + 1) * 128], half


def pack_kv_kernel(k_hbm, v_hbm, kv_ref, k_vmem, v_vmem, sems):
    copies = [
        pltpu.make_async_copy(k_hbm, k_vmem, sems.at[0]),
        pltpu.make_async_copy(v_hbm, v_vmem, sems.at[1]),
    ]
    for copy in copies:
        copy.start()
    for base, copy, ref in ((0, copies[0], k_vmem), (1, copies[1], v_vmem)):
        copy.wait()
        for head, full, half in pack_heads(ref):
            for zs in range(ZS):
                slot = head * ZS + zs
                kv_ref[slot, base * 128 : (base + 1) * 128, :] = full
                kv_ref[slot, 256 + base * 64 : 320 + base * 64, :] = half


def pack_qd_kernel(
    x_ref, q_hbm, c_hbm, pair_hbm, w_hbm, out0, out1, out2, out3,
    q_vmem, c_vmem, pair_vmem, w_vmem, staged, sems,
):
    copies = [
        pltpu.make_async_copy(q_hbm, q_vmem, sems.at[0]),
        pltpu.make_async_copy(c_hbm, c_vmem, sems.at[1]),
        pltpu.make_async_copy(w_hbm, w_vmem, sems.at[2]),
        pltpu.make_async_copy(pair_hbm, pair_vmem, sems.at[3]),
    ]
    for copy in copies:
        copy.start()
    for base, copy, ref in ((0, copies[0], q_vmem), (1, copies[1], c_vmem)):
        copy.wait()
        for head, full, half in pack_heads(ref):
            staged[head, base * 128 : (base + 1) * 128, :] = full
            staged[head, 256 + base * 64 : 320 + base * 64, :] = half
    copies[2].wait()
    copies[3].wait()
    wt = weight_rows(w_vmem[...])
    parts = jnp.concatenate([p.astype(F32) for p in split3(wt)], axis=0).astype(BF)
    pair = pair_vmem[...].reshape(PROW * PAIRS, 128)
    prod = nt(parts, pair)
    bias = (prod[0:8] + (prod[8:16] + prod[16:24])) * (1.0 / SCALE)
    for head in range(HEADS):
        rows = jnp.concatenate(
            [bias[head : head + 1, i * 128 : (i + 1) * 128] for i in range(PROW)], axis=0
        )
        hi = rows.astype(BF).astype(F32)
        staged[head, 384:400, :] = jnp.concatenate([hi, rows - hi], axis=0).astype(BF)
    x = x_ref[0]
    for k, out in enumerate((out0, out1, out2, out3)):
        out[...] = staged[lax.rem(x + k, XS)]


def weight_rows(weight):
    return jnp.concatenate([weight, jnp.zeros((4, 128), F32)], axis=0)


def unpack(full, half, rows_low):
    half = half.astype(F32)
    top = jnp.where(rows_low, half, 0.0)
    bottom = jnp.where(rows_low, roll_half(half), 0.0)
    other = jnp.concatenate([top, bottom], axis=0).astype(BF)
    return full, other


def pack_out(block):
    rest = block[:, 128:]
    return block[:, :128].astype(BF), (rest[:64] + roll_half(rest[64:])).astype(BF)


def loop(steps, body, init):
    return lax.fori_loop(0, steps, body, init, unroll=UNROLL)


def attn_kernel(
    core_ref, x_ref, kv_other, qd0, qd1, qd2, qd3, kv_own, dko_ref, dkx_ref, oq_ref,
    ke, vs, qe, cs, st, ot, dqt, pool, kv_vmem, sem,
):
    low = low_lanes(64)
    core = core_ref[0]
    fetch = pltpu.make_async_copy(kv_other, kv_vmem, sem)
    fetch.start()
    for half, kv_ref in enumerate((kv_own, kv_vmem)):
        if half == 1:
            fetch.wait()
        mine = core if half == 0 else 1 - core
        for m in range(8):
            base = half * 1024 + m * 128
            full, other = unpack(kv_ref[m, 0:128, :], kv_ref[m, 256:320, :], low)
            ke[base : base + 128, 0:128] = full
            ke[base : base + 128, 128:256] = other
            full, other = unpack(kv_ref[m, 128:256, :], kv_ref[m, 320:384, :], low)
            vs[base : base + 128, 0:128] = full
            vs[base : base + 128, 128:256] = other
        row = lax.broadcasted_iota(jnp.int32, (1024, 128), 0)
        col = lax.broadcasted_iota(jnp.int32, (1024, 128), 1)
        cell = lax.shift_right_logical(row, 7) * 16 + mine * 8 + (lax.shift_right_logical(row, 4) & 7)
        table = jnp.where(cell == col, 1.0, 0.0).astype(BF)
        ke[half * 1024 : (half + 1) * 1024, 256:384] = table
        ke[half * 1024 : (half + 1) * 1024, 384:512] = table
    for k, qd_ref in enumerate((qd0, qd1, qd2, qd3)):
        base = k * 128
        full, other = unpack(qd_ref[0:128, :], qd_ref[256:320, :], low)
        qe[base : base + 128, 0:128] = full
        qe[base : base + 128, 128:256] = other
        full, other = unpack(qd_ref[128:256, :], qd_ref[320:384, :], low)
        cs[base : base + 128, 0:128] = full
        cs[base : base + 128, 128:256] = other
        rows = qd_ref[384:400, :].astype(F32)
        for part in range(2):
            wide = jnp.broadcast_to(rows[part * 8 : part * 8 + 8, None, :], (8, POOL, 128))
            qe[base : base + 128, 256 + part * 128 : 384 + part * 128] = wide.reshape(128, 128).astype(BF)

    steps = KROWS // BLOCK

    def scores(b, top):
        at = pl.ds(pl.multiple_of(b * BLOCK, BLOCK), BLOCK)
        s = nt(ke[at, :], qe[...])
        st[at, :] = s
        return jnp.maximum(top, jnp.max(s.reshape(BLOCK // 8, 8, QROWS), axis=0))

    top = loop(steps, scores, jnp.full((8, QROWS), -jnp.inf, F32))
    top = jnp.max(top, axis=0, keepdims=True) * (SCALE * LOG2E)
    ot[...] = jnp.zeros_like(ot)

    def weigh(b, total):
        at = pl.ds(pl.multiple_of(b * BLOCK, BLOCK), BLOCK)
        w = jnp.exp2(st[at, :] * (SCALE * LOG2E) - top)
        st[at, :] = w
        ot[...] += tn(vs[at, :], w.astype(BF))
        return total + jnp.sum(w.reshape(BLOCK // 8, 8, QROWS), axis=0)

    total = loop(steps, weigh, jnp.zeros((8, QROWS), F32))
    inv = 1.0 / jnp.sum(total, axis=0, keepdims=True)
    att = (ot[...] * inv).astype(BF).astype(F32)
    delta = jnp.sum(att * cs[...].astype(F32).T, axis=0, keepdims=True)
    att = att.T
    dqt[...] = jnp.zeros_like(dqt)

    for half, ref in ((0, dko_ref), (1, dkx_ref)):
        mine = core if half == 0 else 1 - core

        def back(b, carry):
            at = pl.ds(pl.multiple_of(half * 1024 + b * BLOCK, BLOCK), BLOCK)
            prob = st[at, :] * inv
            dv = nn(prob.astype(BF), cs[...])
            ds = prob * (nt(vs[at, :], cs[...]) - delta)
            low_ds = ds.astype(BF)
            dk = nn(low_ds, qe[:, 0:256]) * SCALE
            dqt[...] += tn(ke[at, 0:256], low_ds)
            pooled = jnp.sum(ds.reshape(BLOCK // POOL, POOL, QROWS), axis=1)
            for t in range(BLOCK // 128):
                m = b * (BLOCK // 128) + t
                full, rest = pack_out(dk[t * 128 : (t + 1) * 128])
                ref[m, 0:128, :] = full
                ref[m, 256:320, :] = rest
                full, rest = pack_out(dv[t * 128 : (t + 1) * 128])
                ref[m, 128:256, :] = full
                ref[m, 320:384, :] = rest
                pool[pl.ds(pl.multiple_of(m * 16 + mine * 8, 8), 8), :] = pooled[t * 8 : t * 8 + 8]
            return carry

        loop(1024 // BLOCK, back, 0)

    row = lax.broadcasted_iota(jnp.int32, (QROWS // POOL, QROWS), 0)
    col = lax.broadcasted_iota(jnp.int32, (QROWS // POOL, QROWS), 1)
    pick = jnp.where(row == lax.shift_right_logical(col, 4), 1.0, 0.0).astype(BF)
    hi, lo = split2(pool[...])
    grad_bias = nt(pick, hi) + nt(pick, lo)
    dq = dqt[...].T * SCALE
    for k in range(XS):
        to = lax.rem(x_ref[0] + XS - k, XS)
        at = slice(k * 128, (k + 1) * 128)
        full, rest = pack_out(att[at])
        oq_ref[to, 0:128, :] = full
        oq_ref[to, 256:320, :] = rest
        full, rest = pack_out(dq[at])
        oq_ref[to, 128:256, :] = full
        oq_ref[to, 320:384, :] = rest
        rows = grad_bias[k * PROW : (k + 1) * PROW]
        hi = rows.astype(BF).astype(F32)
        oq_ref[to, 384:400, :] = jnp.concatenate([hi, rows - hi], axis=0).astype(BF)


def weight_kernel(oq_ref, pair_ref, out_ref):
    rows = []
    for part in range(2):
        for head in range(HEADS):
            block = oq_ref[head, 384:400, :].astype(F32)[part * 8 : part * 8 + 8]
            rows.append(jnp.concatenate([block[i : i + 1] for i in range(PROW)], axis=1))
    prod = nn(jnp.concatenate(rows, axis=0).astype(BF), pair_ref[...].reshape(PROW * PAIRS, 128))
    out_ref[...] = jnp.broadcast_to((prod[0:4] + prod[4:8])[None], out_ref.shape)


def grads_kernel(
    x_ref, pb, dsb, ke, qe, cs, att_ref, gb_ref, dko_ref, dkx_ref, oq_ref, dqt
):
    dqt[...] = jnp.zeros_like(dqt)
    for half, ref in ((1, dkx_ref), (0, dko_ref)):

        def back(b, carry):
            at = pl.ds(pl.multiple_of(half * 1024 + b * BLOCK, BLOCK), BLOCK)
            low_ds = dsb[at, :]
            dv = nn(pb[at, :], cs[...])
            dk = nn(low_ds, qe[:, 0:256]) * SCALE
            dqt[...] += tn(ke[at, 0:256], low_ds)
            for t in range(BLOCK // 128):
                m = b * (BLOCK // 128) + t
                full, rest = pack_out(dk[t * 128 : (t + 1) * 128])
                ref[m, 0:128, :] = full
                ref[m, 256:320, :] = rest
                full, rest = pack_out(dv[t * 128 : (t + 1) * 128])
                ref[m, 128:256, :] = full
                ref[m, 320:384, :] = rest
            return carry

        lax.fori_loop(0, 1024 // BLOCK, back, 0)

    dq = dqt[...].T * SCALE
    for k in range(XS):
        to = lax.rem(x_ref[0] + XS - k, XS)
        at = slice(k * 128, (k + 1) * 128)
        full, rest = pack_out(att_ref[at, :].astype(F32))
        oq_ref[to, 0:128, :] = full
        oq_ref[to, 256:320, :] = rest
        full, rest = pack_out(dq[at])
        oq_ref[to, 128:256, :] = full
        oq_ref[to, 320:384, :] = rest
        rows = gb_ref[k * PROW : (k + 1) * PROW, :]
        hi = rows.astype(BF).astype(F32)
        oq_ref[to, 384:400, :] = jnp.concatenate([hi, rows - hi], axis=0).astype(BF)


def cores_kernel(z_ref, own_ref, other_ref, send_ref, keep_ref):
    z = z_ref[0]
    for x in range(XS):
        away = x * ZS + 1 - z
        send_ref[x] = (own_ref[away].astype(F32) + other_ref[away].astype(F32)).astype(BF)
        here = x * ZS + z
        keep_ref[x] = own_ref[here].astype(F32) + other_ref[here].astype(F32)


def merge_kernel(x_ref, keep_ref, come_ref, out0, out1, out2, out3):
    for k, out in enumerate((out0, out1, out2, out3)):
        to = lax.rem(x_ref[0] + k, XS)
        out[...] = (keep_ref[to] + come_ref[to].astype(F32)).astype(BF)


def put(ref, fulls, halves):
    low = low_lanes(64)
    for pair in range(2):
        even, odd = halves[2 * pair], halves[2 * pair + 1]
        mid = jnp.concatenate(
            [jnp.where(low, even, roll_half(odd)), jnp.where(low, roll_half(even), odd)], axis=0
        )
        ref[:, (3 * pair) * 128 : (3 * pair + 1) * 128] = fulls[2 * pair].astype(BF)
        ref[:, (3 * pair + 1) * 128 : (3 * pair + 2) * 128] = mid.astype(BF)
        ref[:, (3 * pair + 2) * 128 : (3 * pair + 3) * 128] = fulls[2 * pair + 1].astype(BF)


def query_kernel(oq_ref, w_ref, att_ref, dq_ref, gp_ref):
    for base, ref in ((0, att_ref), (1, dq_ref)):
        put(
            ref,
            [oq_ref[h, base * 128 : (base + 1) * 128, :] for h in range(HEADS)],
            [oq_ref[h, 256 + base * 64 : 320 + base * 64, :].astype(F32) for h in range(HEADS)],
        )
    whi, wmid, _ = split3(w_ref[...])
    wrows = jnp.concatenate([whi.astype(F32), wmid.astype(F32), whi.astype(F32)], axis=0)
    wrows = jnp.concatenate([wrows, jnp.zeros((4, 128), F32)], axis=0).astype(BF)
    blocks = [oq_ref[h, 384:400, :].astype(F32) for h in range(HEADS)]
    zero = jnp.zeros((4, 128), F32)
    for i in range(PROW):
        hi = jnp.concatenate([b[i : i + 1] for b in blocks], axis=0)
        lo = jnp.concatenate([b[8 + i : 9 + i] for b in blocks], axis=0)
        grads = jnp.concatenate([hi, hi, lo, zero], axis=0)
        gp_ref[i] = nn(grads.T.astype(BF), wrows).astype(BF)


def key_kernel(x_ref, in0, in1, in2, in3, far_ref, dk_ref, dv_ref, gw_ref, staged):
    gw_ref[...] = jnp.sum(far_ref[...], axis=0)
    for k, ref in enumerate((in0, in1, in2, in3)):
        staged[lax.rem(x_ref[0] + XS - k, XS)] = ref[...]
    for base, ref in ((0, dk_ref), (1, dv_ref)):
        put(
            ref,
            [staged[h, base * 128 : (base + 1) * 128, :] for h in range(HEADS)],
            [staged[h, 256 + base * 64 : 320 + base * 64, :].astype(F32) for h in range(HEADS)],
        )


def shape(*dims, dtype=BF):
    return jax.ShapeDtypeStruct(dims, dtype)


def call(kernel, out_shape, args, scratch=(), flops=0, moved=0, smem=0, hbm=0, limit=32):
    single = not isinstance(out_shape, tuple)
    rest = len(args) - smem - hbm
    return pl.pallas_call(
        kernel,
        out_shape=out_shape,
        in_specs=[SMEM] * smem + [ANY] * hbm + [VMEM] * rest,
        out_specs=VMEM if single else (VMEM,) * len(out_shape),
        scratch_shapes=list(scratch),
        cost_estimate=pl.CostEstimate(flops=flops, bytes_accessed=moved, transcendentals=0),
        compiler_params=pltpu.CompilerParams(vmem_limit_bytes=limit * 1024 * 1024),
    )(*args)


def attention(*args):
    return call(
        attn_kernel,
        (shape(8, 384, 128), shape(8, 384, 128), shape(XS, 400, 128)),
        args,
        smem=2,
        hbm=1,
        scratch=(
            pltpu.VMEM((KROWS, 512), BF),
            pltpu.VMEM((KROWS, 256), BF),
            pltpu.VMEM((QROWS, 512), BF),
            pltpu.VMEM((QROWS, 256), BF),
            pltpu.VMEM((KROWS, QROWS), F32),
            pltpu.VMEM((256, QROWS), F32),
            pltpu.VMEM((256, QROWS), F32),
            pltpu.VMEM((PAIRS, QROWS), F32),
            pltpu.VMEM((8, 384, 128), BF),
            pltpu.SemaphoreType.DMA(()),
        ),
        flops=8 * 2 * QROWS * KROWS * 256,
        moved=5_000_000,
        limit=32,
    )


def seq_index(x, z, c):
    return (x * ZS + z) * CS + c


def body(dp, queries, keys, values, cotangent, pair, pair_weight):
    xz_groups = [[seq_index(x, z, c) for x in range(XS) for z in range(ZS)] for c in range(CS)]
    x_groups = [[seq_index(x, z, c) for x in range(XS)] for z in range(ZS) for c in range(CS)]
    xc_groups = [[seq_index(x, z, c) for x in range(XS) for c in range(CS)] for z in range(ZS)]
    far_groups = [
        [d * 16 + seq_index(x, z, c) for d in range(dp) for z in range(ZS)]
        for x in range(XS)
        for c in range(CS)
    ]
    across = [
        (seq_index(x, z, c), seq_index(x, 1 - z, c))
        for x in range(XS)
        for z in range(ZS)
        for c in range(CS)
    ]
    swap = [(s, s ^ 1) for s in range(16)]

    def ring(k):
        return [
            (seq_index(x, z, c), seq_index((x + k) % XS, z, c))
            for x in range(XS)
            for z in range(ZS)
            for c in range(CS)
        ]

    place = lax.axis_index("seq").astype(jnp.int32)
    core = (place % CS).reshape(1)
    own_z = (place // CS % ZS).reshape(1)
    own_x = (place // (ZS * CS)).reshape(1)
    pair_rows = pair[0]
    kv = call(
        pack_kv_kernel,
        shape(8, 384, 128),
        (keys[0], values[0]),
        hbm=2,
        scratch=(pltpu.VMEM((TOK, 768), BF), pltpu.VMEM((TOK, 768), BF), pltpu.SemaphoreType.DMA((2,))),
        moved=1_500_000,
        limit=56,
    )
    kv, query_rows, cot_rows = lax.optimization_barrier((kv, queries[0], cotangent[0]))
    kv_own = lax.all_to_all(kv, "seq", 0, 0, axis_index_groups=xz_groups)
    qd = call(
        pack_qd_kernel,
        (shape(400, 128),) * XS,
        (own_x, query_rows, cot_rows, pair_rows, pair_weight.T),
        smem=1,
        hbm=4,
        scratch=(
            pltpu.VMEM((TOK, 768), BF),
            pltpu.VMEM((TOK, 768), BF),
            pltpu.VMEM((PROW, PAIRS, 128), BF),
            pltpu.VMEM((HEADS, 128), F32),
            pltpu.VMEM((HEADS, 400, 128), BF),
            pltpu.SemaphoreType.DMA((4,)),
        ),
        flops=2 * 24 * 1024 * 128,
        moved=1_500_000,
        limit=8,
    )
    qd = [qd[0]] + [lax.ppermute(qd[k], "seq", ring(k)) for k in range(1, XS)]
    kv_own, qd = lax.optimization_barrier((kv_own, qd))
    kv_other = lax.ppermute(kv_own, "seq", swap)
    kv_other = pltpu.with_memory_space_constraint(kv_other, pltpu.MemorySpace.HBM)
    dkv_own, dkv_other, oq = attention(core, own_x, kv_other, *qd, kv_own)
    oq = lax.all_to_all(oq, "seq", 0, 0, axis_index_groups=x_groups)
    dkv_swapped = lax.ppermute(dkv_other, "seq", swap)
    send, keep = call(
        cores_kernel,
        (shape(XS, 384, 128), shape(XS, 384, 128, dtype=F32)),
        (own_z, dkv_own, dkv_swapped),
        smem=1,
        moved=2_400_000,
        limit=8,
    )
    come = lax.ppermute(send, "seq", across)
    total = call(
        weight_kernel, shape(XS * CS, HEADS, 128, dtype=F32), (oq, pair_rows),
        flops=2 * 1024 * 128 * 8, moved=500_000, limit=8,
    )
    total = lax.all_to_all(total, "seq", 0, 0, axis_index_groups=xc_groups).sum(axis=0)
    total, keep = lax.optimization_barrier((total, keep))
    far = jnp.broadcast_to(total[None], (len(far_groups[0]), HEADS, 128))
    far = lax.all_to_all(far, ("dp", "seq"), 0, 0, axis_index_groups=far_groups)
    att, dq, gp = call(
        query_kernel,
        (shape(128, 768), shape(128, 768), shape(PROW, PAIRS, 128)),
        (oq, pair_weight.T),
        flops=2 * 1024 * 128 * 16,
        moved=1_100_000,
        limit=8,
    )
    dkv = call(
        merge_kernel,
        (shape(384, 128),) * XS,
        (own_x, keep, come),
        smem=1,
        moved=1_600_000,
        limit=8,
    )
    dkv = [dkv[0]] + [lax.ppermute(dkv[k], "seq", ring(k)) for k in range(1, XS)]
    dk, dv, gw = call(
        key_kernel,
        (shape(128, 768), shape(128, 768), shape(HEADS, 128, dtype=F32)),
        (own_x, *dkv, far),
        smem=1,
        scratch=(pltpu.VMEM((HEADS, 384, 128), BF),),
        moved=800_000,
        limit=8,
    )
    return att[None], dq[None], dk[None], dv[None], gp[None], gw.T


def solution(mesh):
    rows = P("dp", "seq", None)
    cells = P("dp", "seq", None, None)
    return jax.shard_map(
        functools.partial(body, mesh.shape["dp"]),
        mesh=mesh,
        in_specs=(rows, rows, rows, rows, cells, P()),
        out_specs=(rows, rows, rows, rows, cells, P()),
        check_vma=False,
    )
```

```python
import functools
import math

import jax
import jax.numpy as jnp
from jax import lax
from jax.experimental import pallas as pl
from jax.experimental.pallas import tpu as pltpu
from jax.sharding import PartitionSpec as P

HEADS = 4
HDIM = 192
TOK = 128
POOL = 16
PROW = TOK // POOL
PAIRS = 128
XS = 4
ZS = 2
CS = 2
QROWS = XS * TOK
KROWS = XS * ZS * CS * TOK
HALF = KROWS // CS
PREP = 36
SCALE = HDIM ** (-0.5)
LOG2E = 1.0 / math.log(2.0)
BF = jnp.bfloat16
F32 = jnp.float32
VMEM = pl.BlockSpec(memory_space=pltpu.VMEM)
SMEM = pl.BlockSpec(memory_space=pltpu.SMEM)
ANY = pl.BlockSpec(memory_space=pl.ANY)

FULL_TILE = (0, 2, 3, 5)
HALF_TILE = (1, 1, 4, 4)


def nn(a, b):
    return lax.dot_general(a, b, (((1,), (0,)), ((), ())), preferred_element_type=F32)


def nt(a, b):
    return lax.dot_general(a, b, (((1,), (1,)), ((), ())), preferred_element_type=F32)


def tn(a, b):
    return lax.dot_general(a, b, (((0,), (0,)), ((), ())), preferred_element_type=F32)


def roll_half(x):
    return pltpu.roll(x, 64, 1)


def low_lanes(rows):
    return lax.broadcasted_iota(jnp.int32, (rows, 128), 1) < 64


def split2(x):
    hi = x.astype(BF)
    return hi, (x - hi.astype(F32)).astype(BF)


def split3(x):
    hi = x.astype(BF)
    rest = x - hi.astype(F32)
    mid = rest.astype(BF)
    return hi, mid, (rest - mid.astype(F32)).astype(BF)


def pack_heads(ref):
    low = low_lanes(64)
    for pair in range(2):
        tile = ref[:, (3 * pair + 1) * 128 : (3 * pair + 2) * 128].astype(F32)
        top, bottom = tile[:64], tile[64:]
        even = jnp.where(low, top, roll_half(bottom)).astype(BF)
        odd = jnp.where(low, roll_half(top), bottom).astype(BF)
        for parity, half in ((0, even), (1, odd)):
            head = 2 * pair + parity
            full = FULL_TILE[head]
            yield head, ref[:, full * 128 : (full + 1) * 128], half


def pack_kv_kernel(k_hbm, v_hbm, kv_ref, k_vmem, v_vmem, sems):
    copies = [
        pltpu.make_async_copy(k_hbm, k_vmem, sems.at[0]),
        pltpu.make_async_copy(v_hbm, v_vmem, sems.at[1]),
    ]
    for copy in copies:
        copy.start()
    for base, copy, ref in ((0, copies[0], k_vmem), (1, copies[1], v_vmem)):
        copy.wait()
        for head, full, half in pack_heads(ref):
            for zs in range(ZS):
                slot = head * ZS + zs
                kv_ref[slot, base * 128 : (base + 1) * 128, :] = full
                kv_ref[slot, 256 + base * 64 : 320 + base * 64, :] = half


def pack_qd_kernel(
    x_ref, q_hbm, c_hbm, pair_hbm, w_hbm, out0, out1, out2, out3,
    q_vmem, c_vmem, pair_vmem, w_vmem, staged, sems,
):
    copies = [
        pltpu.make_async_copy(q_hbm, q_vmem, sems.at[0]),
        pltpu.make_async_copy(c_hbm, c_vmem, sems.at[1]),
        pltpu.make_async_copy(w_hbm, w_vmem, sems.at[2]),
        pltpu.make_async_copy(pair_hbm, pair_vmem, sems.at[3]),
    ]
    for copy in copies:
        copy.start()
    for base, copy, ref in ((0, copies[0], q_vmem), (1, copies[1], c_vmem)):
        copy.wait()
        for head, full, half in pack_heads(ref):
            staged[head, base * 128 : (base + 1) * 128, :] = full
            staged[head, 256 + base * 64 : 320 + base * 64, :] = half
    copies[2].wait()
    copies[3].wait()
    wt = weight_rows(w_vmem[...])
    parts = jnp.concatenate([p.astype(F32) for p in split3(wt)], axis=0).astype(BF)
    pair = pair_vmem[...].reshape(PROW * PAIRS, 128)
    prod = nt(parts, pair)
    bias = (prod[0:8] + (prod[8:16] + prod[16:24])) * (1.0 / SCALE)
    for head in range(HEADS):
        rows = jnp.concatenate(
            [bias[head : head + 1, i * 128 : (i + 1) * 128] for i in range(PROW)], axis=0
        )
        hi = rows.astype(BF).astype(F32)
        staged[head, 384:400, :] = jnp.concatenate([hi, rows - hi], axis=0).astype(BF)
    x = x_ref[0]
    for k, out in enumerate((out0, out1, out2, out3)):
        out[...] = staged[lax.rem(x + k, XS)]


def weight_rows(weight):
    return jnp.concatenate([weight, jnp.zeros((4, 128), F32)], axis=0)


def unpack(full, half, rows_low):
    half = half.astype(F32)
    top = jnp.where(rows_low, half, 0.0)
    bottom = jnp.where(rows_low, roll_half(half), 0.0)
    other = jnp.concatenate([top, bottom], axis=0).astype(BF)
    return full, other


def pack_out(block):
    rest = block[:, 128:]
    return block[:, :128].astype(BF), (rest[:64] + roll_half(rest[64:])).astype(BF)


def unpack_keys(kv_ref, mine, ke, vs):
    low = low_lanes(64)
    for m in range(8):
        rows = slice(m * 128, (m + 1) * 128)
        full, other = unpack(kv_ref[m, 0:128, :], kv_ref[m, 256:320, :], low)
        ke[rows, 0:128] = full
        ke[rows, 128:256] = other
        full, other = unpack(kv_ref[m, 128:256, :], kv_ref[m, 320:384, :], low)
        vs[rows, 0:128] = full
        vs[rows, 128:256] = other
    row = lax.broadcasted_iota(jnp.int32, (HALF, 128), 0)
    col = lax.broadcasted_iota(jnp.int32, (HALF, 128), 1)
    cell = lax.shift_right_logical(row, 7) * 16 + mine * 8 + (lax.shift_right_logical(row, 4) & 7)
    table = jnp.where(cell == col, 1.0, 0.0).astype(BF)
    ke[:, 256:384] = table
    ke[:, 384:512] = table


def prepare_kernel(core_ref, qd0, qd1, qd2, qd3, kv_own, ke, vs, qe, cs, st, top_ref):
    low = low_lanes(64)
    unpack_keys(kv_own, core_ref[0], ke, vs)
    for k, qd_ref in enumerate((qd0, qd1, qd2, qd3)):
        base = k * 128
        full, other = unpack(qd_ref[0:128, :], qd_ref[256:320, :], low)
        qe[base : base + 128, 0:128] = full
        qe[base : base + 128, 128:256] = other
        full, other = unpack(qd_ref[128:256, :], qd_ref[320:384, :], low)
        cs[base : base + 128, 0:128] = full
        cs[base : base + 128, 128:256] = other
        rows = qd_ref[384:400, :].astype(F32)
        for part in range(2):
            wide = jnp.broadcast_to(rows[part * 8 : part * 8 + 8, None, :], (8, POOL, 128))
            qe[base : base + 128, 256 + part * 128 : 384 + part * 128] = wide.reshape(128, 128).astype(BF)
    s = nt(ke[...], qe[...])
    st[...] = s
    top_ref[...] = jnp.max(s.reshape(HALF // 8, 8, QROWS), axis=0)


def attn_kernel(
    core_ref, x_ref, kv_other, ke_own, vs_own, qe, cs, st_own, top_ref, dko_ref, dkx_ref, oq_ref,
    ke_other, vs_other, st, ot, dqt, pool,
):
    core = core_ref[0]
    unpack_keys(kv_other, 1 - core, ke_other, vs_other)
    halves = ((ke_own, vs_own, core, dko_ref), (ke_other, vs_other, 1 - core, dkx_ref))
    s = nt(ke_other[...], qe[...])
    st[HALF:, :] = s
    top = jnp.maximum(top_ref[...], jnp.max(s.reshape(HALF // 8, 8, QROWS), axis=0))
    top = jnp.max(top, axis=0, keepdims=True) * (SCALE * LOG2E)
    total = jnp.zeros((8, QROWS), F32)
    for half, (_, vs, _, _) in enumerate(halves):
        at = slice(half * HALF, (half + 1) * HALF)
        s = st_own[...] if half == 0 else st[at, :]
        w = jnp.exp2(s * (SCALE * LOG2E) - top)
        st[at, :] = w
        part = tn(vs[...], w.astype(BF))
        ot[...] = part if half == 0 else ot[...] + part
        total += jnp.sum(w.reshape(HALF // 8, 8, QROWS), axis=0)
    inv = 1.0 / jnp.sum(total, axis=0, keepdims=True)
    att = (ot[...] * inv).astype(BF).astype(F32)
    delta = jnp.sum(att * cs[...].astype(F32).T, axis=0, keepdims=True)
    att = att.T
    for half, (ke, vs, mine, ref) in enumerate(halves):
        prob = st[half * HALF : (half + 1) * HALF, :] * inv
        dv = nn(prob.astype(BF), cs[...])
        ds = prob * (nt(vs[...], cs[...]) - delta)
        low_ds = ds.astype(BF)
        dk = nn(low_ds, qe[:, 0:256]) * SCALE
        part = tn(ke[:, 0:256], low_ds)
        dqt[...] = part if half == 0 else dqt[...] + part
        pooled = jnp.sum(ds.reshape(HALF // POOL, POOL, QROWS), axis=1)
        for m in range(8):
            rows = slice(m * 128, (m + 1) * 128)
            full, rest = pack_out(dk[rows])
            ref[m, 0:128, :] = full
            ref[m, 256:320, :] = rest
            full, rest = pack_out(dv[rows])
            ref[m, 128:256, :] = full
            ref[m, 320:384, :] = rest
            pool[pl.ds(pl.multiple_of(m * 16 + mine * 8, 8), 8), :] = pooled[m * 8 : m * 8 + 8]

    row = lax.broadcasted_iota(jnp.int32, (QROWS // POOL, QROWS), 0)
    col = lax.broadcasted_iota(jnp.int32, (QROWS // POOL, QROWS), 1)
    pick = jnp.where(row == lax.shift_right_logical(col, 4), 1.0, 0.0).astype(BF)
    hi, lo = split2(pool[...])
    grad_bias = nt(pick, hi) + nt(pick, lo)
    dq = dqt[...].T * SCALE
    for k in range(XS):
        to = lax.rem(x_ref[0] + XS - k, XS)
        at = slice(k * 128, (k + 1) * 128)
        full, rest = pack_out(att[at])
        oq_ref[to, 0:128, :] = full
        oq_ref[to, 256:320, :] = rest
        full, rest = pack_out(dq[at])
        oq_ref[to, 128:256, :] = full
        oq_ref[to, 320:384, :] = rest
        rows = grad_bias[k * PROW : (k + 1) * PROW]
        hi = rows.astype(BF).astype(F32)
        oq_ref[to, 384:400, :] = jnp.concatenate([hi, rows - hi], axis=0).astype(BF)


def weight_kernel(oq_ref, pair_ref, out_ref):
    rows = []
    for part in range(2):
        for head in range(HEADS):
            block = oq_ref[head, 384:400, :].astype(F32)[part * 8 : part * 8 + 8]
            rows.append(jnp.concatenate([block[i : i + 1] for i in range(PROW)], axis=1))
    prod = nn(jnp.concatenate(rows, axis=0).astype(BF), pair_ref[...].reshape(PROW * PAIRS, 128))
    out_ref[...] = jnp.broadcast_to((prod[0:4] + prod[4:8])[None], out_ref.shape)


def grads_kernel(
    x_ref, pb, dsb, ke, qe, cs, att_ref, gb_ref, dko_ref, dkx_ref, oq_ref, dqt
):
    dqt[...] = jnp.zeros_like(dqt)
    for half, ref in ((1, dkx_ref), (0, dko_ref)):

        def back(b, carry):
            at = pl.ds(pl.multiple_of(half * 1024 + b * BLOCK, BLOCK), BLOCK)
            low_ds = dsb[at, :]
            dv = nn(pb[at, :], cs[...])
            dk = nn(low_ds, qe[:, 0:256]) * SCALE
            dqt[...] += tn(ke[at, 0:256], low_ds)
            for t in range(BLOCK // 128):
                m = b * (BLOCK // 128) + t
                full, rest = pack_out(dk[t * 128 : (t + 1) * 128])
                ref[m, 0:128, :] = full
                ref[m, 256:320, :] = rest
                full, rest = pack_out(dv[t * 128 : (t + 1) * 128])
                ref[m, 128:256, :] = full
                ref[m, 320:384, :] = rest
            return carry

        lax.fori_loop(0, 1024 // BLOCK, back, 0)

    dq = dqt[...].T * SCALE
    for k in range(XS):
        to = lax.rem(x_ref[0] + XS - k, XS)
        at = slice(k * 128, (k + 1) * 128)
        full, rest = pack_out(att_ref[at, :].astype(F32))
        oq_ref[to, 0:128, :] = full
        oq_ref[to, 256:320, :] = rest
        full, rest = pack_out(dq[at])
        oq_ref[to, 128:256, :] = full
        oq_ref[to, 320:384, :] = rest
        rows = gb_ref[k * PROW : (k + 1) * PROW, :]
        hi = rows.astype(BF).astype(F32)
        oq_ref[to, 384:400, :] = jnp.concatenate([hi, rows - hi], axis=0).astype(BF)


def cores_kernel(z_ref, own_ref, other_ref, send_ref, keep_ref):
    z = z_ref[0]
    for x in range(XS):
        away = x * ZS + 1 - z
        send_ref[x] = (own_ref[away].astype(F32) + other_ref[away].astype(F32)).astype(BF)
        here = x * ZS + z
        keep_ref[x] = own_ref[here].astype(F32) + other_ref[here].astype(F32)


def merge_kernel(x_ref, keep_ref, come_ref, out0, out1, out2, out3):
    for k, out in enumerate((out0, out1, out2, out3)):
        to = lax.rem(x_ref[0] + k, XS)
        out[...] = (keep_ref[to] + come_ref[to].astype(F32)).astype(BF)


def put(ref, fulls, halves):
    low = low_lanes(64)
    for pair in range(2):
        even, odd = halves[2 * pair], halves[2 * pair + 1]
        mid = jnp.concatenate(
            [jnp.where(low, even, roll_half(odd)), jnp.where(low, roll_half(even), odd)], axis=0
        )
        ref[:, (3 * pair) * 128 : (3 * pair + 1) * 128] = fulls[2 * pair].astype(BF)
        ref[:, (3 * pair + 1) * 128 : (3 * pair + 2) * 128] = mid.astype(BF)
        ref[:, (3 * pair + 2) * 128 : (3 * pair + 3) * 128] = fulls[2 * pair + 1].astype(BF)


def query_kernel(oq_ref, w_ref, att_ref, dq_ref, gp_ref):
    for base, ref in ((0, att_ref), (1, dq_ref)):
        put(
            ref,
            [oq_ref[h, base * 128 : (base + 1) * 128, :] for h in range(HEADS)],
            [oq_ref[h, 256 + base * 64 : 320 + base * 64, :].astype(F32) for h in range(HEADS)],
        )
    whi, wmid, _ = split3(w_ref[...])
    wrows = jnp.concatenate([whi.astype(F32), wmid.astype(F32), whi.astype(F32)], axis=0)
    wrows = jnp.concatenate([wrows, jnp.zeros((4, 128), F32)], axis=0).astype(BF)
    blocks = [oq_ref[h, 384:400, :].astype(F32) for h in range(HEADS)]
    zero = jnp.zeros((4, 128), F32)
    for i in range(PROW):
        hi = jnp.concatenate([b[i : i + 1] for b in blocks], axis=0)
        lo = jnp.concatenate([b[8 + i : 9 + i] for b in blocks], axis=0)
        grads = jnp.concatenate([hi, hi, lo, zero], axis=0)
        gp_ref[i] = nn(grads.T.astype(BF), wrows).astype(BF)


def key_kernel(x_ref, in0, in1, in2, in3, far_ref, dk_ref, dv_ref, gw_ref, staged):
    gw_ref[...] = jnp.sum(far_ref[...], axis=0)
    for k, ref in enumerate((in0, in1, in2, in3)):
        staged[lax.rem(x_ref[0] + XS - k, XS)] = ref[...]
    for base, ref in ((0, dk_ref), (1, dv_ref)):
        put(
            ref,
            [staged[h, base * 128 : (base + 1) * 128, :] for h in range(HEADS)],
            [staged[h, 256 + base * 64 : 320 + base * 64, :].astype(F32) for h in range(HEADS)],
        )


def shape(*dims, dtype=BF):
    return jax.ShapeDtypeStruct(dims, dtype)


def call(kernel, out_shape, args, scratch=(), flops=0, moved=0, smem=0, hbm=0, limit=32):
    single = not isinstance(out_shape, tuple)
    rest = len(args) - smem - hbm
    return pl.pallas_call(
        kernel,
        out_shape=out_shape,
        in_specs=[SMEM] * smem + [ANY] * hbm + [VMEM] * rest,
        out_specs=VMEM if single else (VMEM,) * len(out_shape),
        scratch_shapes=list(scratch),
        cost_estimate=pl.CostEstimate(flops=flops, bytes_accessed=moved, transcendentals=0),
        compiler_params=pltpu.CompilerParams(vmem_limit_bytes=limit * 1024 * 1024),
    )(*args)


def prepare(*args):
    return call(
        prepare_kernel,
        (
            shape(HALF, 512), shape(HALF, 256), shape(QROWS, 512), shape(QROWS, 256),
            shape(HALF, QROWS, dtype=F32), shape(8, QROWS, dtype=F32),
        ),
        args,
        smem=1,
        flops=2 * QROWS * KROWS * 256,
        moved=6_000_000,
        limit=PREP,
    )


def attention(*args):
    return call(
        attn_kernel,
        (shape(8, 384, 128), shape(8, 384, 128), shape(XS, 400, 128)),
        args,
        smem=2,
        scratch=(
            pltpu.VMEM((HALF, 512), BF),
            pltpu.VMEM((HALF, 256), BF),
            pltpu.VMEM((KROWS, QROWS), F32),
            pltpu.VMEM((256, QROWS), F32),
            pltpu.VMEM((256, QROWS), F32),
            pltpu.VMEM((PAIRS, QROWS), F32),
        ),
        flops=7 * 2 * QROWS * KROWS * 256,
        moved=8_000_000,
        limit=28,
    )


def seq_index(x, z, c):
    return (x * ZS + z) * CS + c


def body(dp, queries, keys, values, cotangent, pair, pair_weight):
    xz_groups = [[seq_index(x, z, c) for x in range(XS) for z in range(ZS)] for c in range(CS)]
    x_groups = [[seq_index(x, z, c) for x in range(XS)] for z in range(ZS) for c in range(CS)]
    xc_groups = [[seq_index(x, z, c) for x in range(XS) for c in range(CS)] for z in range(ZS)]
    far_groups = [
        [d * 16 + seq_index(x, z, c) for d in range(dp) for z in range(ZS)]
        for x in range(XS)
        for c in range(CS)
    ]
    across = [
        (seq_index(x, z, c), seq_index(x, 1 - z, c))
        for x in range(XS)
        for z in range(ZS)
        for c in range(CS)
    ]
    swap = [(s, s ^ 1) for s in range(16)]

    def ring(k):
        return [
            (seq_index(x, z, c), seq_index((x + k) % XS, z, c))
            for x in range(XS)
            for z in range(ZS)
            for c in range(CS)
        ]

    place = lax.axis_index("seq").astype(jnp.int32)
    core = (place % CS).reshape(1)
    own_z = (place // CS % ZS).reshape(1)
    own_x = (place // (ZS * CS)).reshape(1)
    pair_rows = pair[0]
    kv = call(
        pack_kv_kernel,
        shape(8, 384, 128),
        (keys[0], values[0]),
        hbm=2,
        scratch=(pltpu.VMEM((TOK, 768), BF), pltpu.VMEM((TOK, 768), BF), pltpu.SemaphoreType.DMA((2,))),
        moved=1_500_000,
        limit=56,
    )
    kv, query_rows, cot_rows = lax.optimization_barrier((kv, queries[0], cotangent[0]))
    kv_own = lax.all_to_all(kv, "seq", 0, 0, axis_index_groups=xz_groups)
    qd = call(
        pack_qd_kernel,
        (shape(400, 128),) * XS,
        (own_x, query_rows, cot_rows, pair_rows, pair_weight.T),
        smem=1,
        hbm=4,
        scratch=(
            pltpu.VMEM((TOK, 768), BF),
            pltpu.VMEM((TOK, 768), BF),
            pltpu.VMEM((PROW, PAIRS, 128), BF),
            pltpu.VMEM((HEADS, 128), F32),
            pltpu.VMEM((HEADS, 400, 128), BF),
            pltpu.SemaphoreType.DMA((4,)),
        ),
        flops=2 * 24 * 1024 * 128,
        moved=1_500_000,
        limit=8,
    )
    qd = [qd[0]] + [lax.ppermute(qd[k], "seq", ring(k)) for k in range(1, XS)]
    kv_own, qd = lax.optimization_barrier((kv_own, qd))
    kv_other = lax.ppermute(kv_own, "seq", swap)
    ready = prepare(core, *qd, kv_own)
    dkv_own, dkv_other, oq = attention(core, own_x, kv_other, *ready)
    oq = lax.all_to_all(oq, "seq", 0, 0, axis_index_groups=x_groups)
    dkv_swapped = lax.ppermute(dkv_other, "seq", swap)
    send, keep = call(
        cores_kernel,
        (shape(XS, 384, 128), shape(XS, 384, 128, dtype=F32)),
        (own_z, dkv_own, dkv_swapped),
        smem=1,
        moved=2_400_000,
        limit=8,
    )
    come = lax.ppermute(send, "seq", across)
    total = call(
        weight_kernel, shape(XS * CS, HEADS, 128, dtype=F32), (oq, pair_rows),
        flops=2 * 1024 * 128 * 8, moved=500_000, limit=8,
    )
    total = lax.all_to_all(total, "seq", 0, 0, axis_index_groups=xc_groups).sum(axis=0)
    total, keep = lax.optimization_barrier((total, keep))
    far = jnp.broadcast_to(total[None], (len(far_groups[0]), HEADS, 128))
    far = lax.all_to_all(far, ("dp", "seq"), 0, 0, axis_index_groups=far_groups)
    att, dq, gp = call(
        query_kernel,
        (shape(128, 768), shape(128, 768), shape(PROW, PAIRS, 128)),
        (oq, pair_weight.T),
        flops=2 * 1024 * 128 * 16,
        moved=1_100_000,
        limit=8,
    )
    dkv = call(
        merge_kernel,
        (shape(384, 128),) * XS,
        (own_x, keep, come),
        smem=1,
        moved=1_600_000,
        limit=8,
    )
    dkv = [dkv[0]] + [lax.ppermute(dkv[k], "seq", ring(k)) for k in range(1, XS)]
    dk, dv, gw = call(
        key_kernel,
        (shape(128, 768), shape(128, 768), shape(HEADS, 128, dtype=F32)),
        (own_x, *dkv, far),
        smem=1,
        scratch=(pltpu.VMEM((HEADS, 384, 128), BF),),
        moved=800_000,
        limit=8,
    )
    return att[None], dq[None], dk[None], dv[None], gp[None], gw.T


def solution(mesh):
    rows = P("dp", "seq", None)
    cells = P("dp", "seq", None, None)
    return jax.shard_map(
        functools.partial(body, mesh.shape["dp"]),
        mesh=mesh,
        in_specs=(rows, rows, rows, rows, cells, P()),
        out_specs=(rows, rows, rows, rows, cells, P()),
        check_vma=False,
    )
```

```python
import functools
import math

import jax
import jax.numpy as jnp
from jax import lax
from jax.experimental import pallas as pl
from jax.experimental.pallas import tpu as pltpu
from jax.sharding import PartitionSpec as P

HEADS = 4
HDIM = 192
TOK = 128
POOL = 16
PROW = TOK // POOL
PAIRS = 128
XS = 4
ZS = 2
CS = 2
QROWS = XS * TOK
KROWS = XS * ZS * CS * TOK
HALF = KROWS // CS
PREP = 36
SCALE = HDIM ** (-0.5)
LOG2E = 1.0 / math.log(2.0)
BF = jnp.bfloat16
F32 = jnp.float32
VMEM = pl.BlockSpec(memory_space=pltpu.VMEM)
SMEM = pl.BlockSpec(memory_space=pltpu.SMEM)
ANY = pl.BlockSpec(memory_space=pl.ANY)

FULL_TILE = (0, 2, 3, 5)
HALF_TILE = (1, 1, 4, 4)


def nn(a, b):
    return lax.dot_general(a, b, (((1,), (0,)), ((), ())), preferred_element_type=F32)


def nt(a, b):
    return lax.dot_general(a, b, (((1,), (1,)), ((), ())), preferred_element_type=F32)


def tn(a, b):
    return lax.dot_general(a, b, (((0,), (0,)), ((), ())), preferred_element_type=F32)


def roll_half(x):
    return pltpu.roll(x, 64, 1)


def low_lanes(rows):
    return lax.broadcasted_iota(jnp.int32, (rows, 128), 1) < 64


def split2(x):
    hi = x.astype(BF)
    return hi, (x - hi.astype(F32)).astype(BF)


def split3(x):
    hi = x.astype(BF)
    rest = x - hi.astype(F32)
    mid = rest.astype(BF)
    return hi, mid, (rest - mid.astype(F32)).astype(BF)


def pack_heads(ref):
    low = low_lanes(64)
    for pair in range(2):
        tile = ref[:, (3 * pair + 1) * 128 : (3 * pair + 2) * 128].astype(F32)
        top, bottom = tile[:64], tile[64:]
        even = jnp.where(low, top, roll_half(bottom)).astype(BF)
        odd = jnp.where(low, roll_half(top), bottom).astype(BF)
        for parity, half in ((0, even), (1, odd)):
            head = 2 * pair + parity
            full = FULL_TILE[head]
            yield head, ref[:, full * 128 : (full + 1) * 128], half


def pack_kv_kernel(k_hbm, v_hbm, kv_ref, k_vmem, v_vmem, sems):
    copies = [
        pltpu.make_async_copy(k_hbm, k_vmem, sems.at[0]),
        pltpu.make_async_copy(v_hbm, v_vmem, sems.at[1]),
    ]
    for copy in copies:
        copy.start()
    for base, copy, ref in ((0, copies[0], k_vmem), (1, copies[1], v_vmem)):
        copy.wait()
        for head, full, half in pack_heads(ref):
            for zs in range(ZS):
                slot = head * ZS + zs
                kv_ref[slot, base * 128 : (base + 1) * 128, :] = full
                kv_ref[slot, 256 + base * 64 : 320 + base * 64, :] = half


def pack_qd_kernel(
    x_ref, q_hbm, c_hbm, pair_hbm, w_hbm, out0, out1, out2, out3,
    q_vmem, c_vmem, pair_vmem, w_vmem, staged, sems,
):
    copies = [
        pltpu.make_async_copy(q_hbm, q_vmem, sems.at[0]),
        pltpu.make_async_copy(c_hbm, c_vmem, sems.at[1]),
        pltpu.make_async_copy(w_hbm, w_vmem, sems.at[2]),
        pltpu.make_async_copy(pair_hbm, pair_vmem, sems.at[3]),
    ]
    for copy in copies:
        copy.start()
    for base, copy, ref in ((0, copies[0], q_vmem), (1, copies[1], c_vmem)):
        copy.wait()
        for head, full, half in pack_heads(ref):
            staged[head, base * 128 : (base + 1) * 128, :] = full
            staged[head, 256 + base * 64 : 320 + base * 64, :] = half
    copies[2].wait()
    copies[3].wait()
    wt = weight_rows(w_vmem[...])
    parts = jnp.concatenate([p.astype(F32) for p in split3(wt)], axis=0).astype(BF)
    pair = pair_vmem[...].reshape(PROW * PAIRS, 128)
    prod = nt(parts, pair)
    bias = (prod[0:8] + (prod[8:16] + prod[16:24])) * (1.0 / SCALE)
    for head in range(HEADS):
        rows = jnp.concatenate(
            [bias[head : head + 1, i * 128 : (i + 1) * 128] for i in range(PROW)], axis=0
        )
        hi = rows.astype(BF).astype(F32)
        staged[head, 384:400, :] = jnp.concatenate([hi, rows - hi], axis=0).astype(BF)
    x = x_ref[0]
    for k, out in enumerate((out0, out1, out2, out3)):
        out[...] = staged[lax.rem(x + k, XS)]


def weight_rows(weight):
    return jnp.concatenate([weight, jnp.zeros((4, 128), F32)], axis=0)


def unpack(full, half, rows_low):
    half = half.astype(F32)
    top = jnp.where(rows_low, half, 0.0)
    bottom = jnp.where(rows_low, roll_half(half), 0.0)
    other = jnp.concatenate([top, bottom], axis=0).astype(BF)
    return full, other


def pack_out(block):
    rest = block[:, 128:]
    return block[:, :128].astype(BF), (rest[:64] + roll_half(rest[64:])).astype(BF)


def unpack_keys(kv_ref, mine, ke, vs):
    low = low_lanes(64)
    for m in range(8):
        rows = slice(m * 128, (m + 1) * 128)
        full, other = unpack(kv_ref[m, 0:128, :], kv_ref[m, 256:320, :], low)
        ke[rows, 0:128] = full
        ke[rows, 128:256] = other
        full, other = unpack(kv_ref[m, 128:256, :], kv_ref[m, 320:384, :], low)
        vs[rows, 0:128] = full
        vs[rows, 128:256] = other
    row = lax.broadcasted_iota(jnp.int32, (HALF, 128), 0)
    col = lax.broadcasted_iota(jnp.int32, (HALF, 128), 1)
    cell = lax.shift_right_logical(row, 7) * 16 + mine * 8 + (lax.shift_right_logical(row, 4) & 7)
    table = jnp.where(cell == col, 1.0, 0.0).astype(BF)
    ke[:, 256:384] = table
    ke[:, 384:512] = table


def soften(ke, vs, qe, st):
    s = nt(ke[...], qe[...])
    top = jnp.max(jnp.max(s.reshape(HALF // 8, 8, QROWS), axis=0), axis=0, keepdims=True)
    top = top * (SCALE * LOG2E)
    w = jnp.exp2(s * (SCALE * LOG2E) - top)
    st[...] = w
    total = jnp.sum(w.reshape(HALF // 8, 8, QROWS), axis=0)
    return top, total, tn(vs[...], w.astype(BF))


def prepare_kernel(
    core_ref, qd0, qd1, qd2, qd3, kv_own, ke, vs, qe, cs, st, top_ref, total_ref, ot_ref
):
    low = low_lanes(64)
    unpack_keys(kv_own, core_ref[0], ke, vs)
    for k, qd_ref in enumerate((qd0, qd1, qd2, qd3)):
        base = k * 128
        full, other = unpack(qd_ref[0:128, :], qd_ref[256:320, :], low)
        qe[base : base + 128, 0:128] = full
        qe[base : base + 128, 128:256] = other
        full, other = unpack(qd_ref[128:256, :], qd_ref[320:384, :], low)
        cs[base : base + 128, 0:128] = full
        cs[base : base + 128, 128:256] = other
        rows = qd_ref[384:400, :].astype(F32)
        for part in range(2):
            wide = jnp.broadcast_to(rows[part * 8 : part * 8 + 8, None, :], (8, POOL, 128))
            qe[base : base + 128, 256 + part * 128 : 384 + part * 128] = wide.reshape(128, 128).astype(BF)
    top, total_ref[...], ot_ref[...] = soften(ke, vs, qe, st)
    top_ref[...] = jnp.broadcast_to(top, top_ref.shape)


def attn_kernel(
    core_ref, x_ref, kv_other, ke_own, vs_own, qe, cs, st_own, top_ref, total_ref, ot_ref,
    dko_ref, dkx_ref, oq_ref, ke_other, vs_other, st_other, dqt, pool,
):
    core = core_ref[0]
    unpack_keys(kv_other, 1 - core, ke_other, vs_other)
    top_other, total_other, ot_other = soften(ke_other, vs_other, qe, st_other)
    top_own = top_ref[0:1, :]
    top = jnp.maximum(top_own, top_other)
    own, other = jnp.exp2(top_own - top), jnp.exp2(top_other - top)
    total = total_ref[...] * own + total_other * other
    inv = 1.0 / jnp.sum(total, axis=0, keepdims=True)
    halves = (
        (ke_own, vs_own, st_own, own * inv, core, dko_ref),
        (ke_other, vs_other, st_other, other * inv, 1 - core, dkx_ref),
    )
    ot = ot_ref[...] * own + ot_other * other
    att = (ot * inv).astype(BF).astype(F32)
    delta = jnp.sum(att * cs[...].astype(F32).T, axis=0, keepdims=True)
    att = att.T
    for half, (ke, vs, st, share, mine, ref) in enumerate(halves):
        prob = st[...] * share
        dv = nn(prob.astype(BF), cs[...])
        ds = prob * (nt(vs[...], cs[...]) - delta)
        low_ds = ds.astype(BF)
        dk = nn(low_ds, qe[:, 0:256]) * SCALE
        part = tn(ke[:, 0:256], low_ds)
        dqt[...] = part if half == 0 else dqt[...] + part
        pooled = jnp.sum(ds.reshape(HALF // POOL, POOL, QROWS), axis=1)
        for m in range(8):
            rows = slice(m * 128, (m + 1) * 128)
            full, rest = pack_out(dk[rows])
            ref[m, 0:128, :] = full
            ref[m, 256:320, :] = rest
            full, rest = pack_out(dv[rows])
            ref[m, 128:256, :] = full
            ref[m, 320:384, :] = rest
            pool[pl.ds(pl.multiple_of(m * 16 + mine * 8, 8), 8), :] = pooled[m * 8 : m * 8 + 8]

    row = lax.broadcasted_iota(jnp.int32, (QROWS // POOL, QROWS), 0)
    col = lax.broadcasted_iota(jnp.int32, (QROWS // POOL, QROWS), 1)
    pick = jnp.where(row == lax.shift_right_logical(col, 4), 1.0, 0.0).astype(BF)
    hi, lo = split2(pool[...])
    grad_bias = nt(pick, hi) + nt(pick, lo)
    dq = dqt[...].T * SCALE
    for k in range(XS):
        to = lax.rem(x_ref[0] + XS - k, XS)
        at = slice(k * 128, (k + 1) * 128)
        full, rest = pack_out(att[at])
        oq_ref[to, 0:128, :] = full
        oq_ref[to, 256:320, :] = rest
        full, rest = pack_out(dq[at])
        oq_ref[to, 128:256, :] = full
        oq_ref[to, 320:384, :] = rest
        rows = grad_bias[k * PROW : (k + 1) * PROW]
        hi = rows.astype(BF).astype(F32)
        oq_ref[to, 384:400, :] = jnp.concatenate([hi, rows - hi], axis=0).astype(BF)


def weight_kernel(oq_ref, pair_ref, out_ref):
    rows = []
    for part in range(2):
        for head in range(HEADS):
            block = oq_ref[head, 384:400, :].astype(F32)[part * 8 : part * 8 + 8]
            rows.append(jnp.concatenate([block[i : i + 1] for i in range(PROW)], axis=1))
    prod = nn(jnp.concatenate(rows, axis=0).astype(BF), pair_ref[...].reshape(PROW * PAIRS, 128))
    out_ref[...] = jnp.broadcast_to((prod[0:4] + prod[4:8])[None], out_ref.shape)


def grads_kernel(
    x_ref, pb, dsb, ke, qe, cs, att_ref, gb_ref, dko_ref, dkx_ref, oq_ref, dqt
):
    dqt[...] = jnp.zeros_like(dqt)
    for half, ref in ((1, dkx_ref), (0, dko_ref)):

        def back(b, carry):
            at = pl.ds(pl.multiple_of(half * 1024 + b * BLOCK, BLOCK), BLOCK)
            low_ds = dsb[at, :]
            dv = nn(pb[at, :], cs[...])
            dk = nn(low_ds, qe[:, 0:256]) * SCALE
            dqt[...] += tn(ke[at, 0:256], low_ds)
            for t in range(BLOCK // 128):
                m = b * (BLOCK // 128) + t
                full, rest = pack_out(dk[t * 128 : (t + 1) * 128])
                ref[m, 0:128, :] = full
                ref[m, 256:320, :] = rest
                full, rest = pack_out(dv[t * 128 : (t + 1) * 128])
                ref[m, 128:256, :] = full
                ref[m, 320:384, :] = rest
            return carry

        lax.fori_loop(0, 1024 // BLOCK, back, 0)

    dq = dqt[...].T * SCALE
    for k in range(XS):
        to = lax.rem(x_ref[0] + XS - k, XS)
        at = slice(k * 128, (k + 1) * 128)
        full, rest = pack_out(att_ref[at, :].astype(F32))
        oq_ref[to, 0:128, :] = full
        oq_ref[to, 256:320, :] = rest
        full, rest = pack_out(dq[at])
        oq_ref[to, 128:256, :] = full
        oq_ref[to, 320:384, :] = rest
        rows = gb_ref[k * PROW : (k + 1) * PROW, :]
        hi = rows.astype(BF).astype(F32)
        oq_ref[to, 384:400, :] = jnp.concatenate([hi, rows - hi], axis=0).astype(BF)


def cores_kernel(z_ref, own_ref, other_ref, send_ref, keep_ref):
    z = z_ref[0]
    for x in range(XS):
        away = x * ZS + 1 - z
        send_ref[x] = (own_ref[away].astype(F32) + other_ref[away].astype(F32)).astype(BF)
        here = x * ZS + z
        keep_ref[x] = own_ref[here].astype(F32) + other_ref[here].astype(F32)


def merge_kernel(x_ref, keep_ref, come_ref, out0, out1, out2, out3):
    for k, out in enumerate((out0, out1, out2, out3)):
        to = lax.rem(x_ref[0] + k, XS)
        out[...] = (keep_ref[to] + come_ref[to].astype(F32)).astype(BF)


def put(ref, fulls, halves):
    low = low_lanes(64)
    for pair in range(2):
        even, odd = halves[2 * pair], halves[2 * pair + 1]
        mid = jnp.concatenate(
            [jnp.where(low, even, roll_half(odd)), jnp.where(low, roll_half(even), odd)], axis=0
        )
        ref[:, (3 * pair) * 128 : (3 * pair + 1) * 128] = fulls[2 * pair].astype(BF)
        ref[:, (3 * pair + 1) * 128 : (3 * pair + 2) * 128] = mid.astype(BF)
        ref[:, (3 * pair + 2) * 128 : (3 * pair + 3) * 128] = fulls[2 * pair + 1].astype(BF)


def query_kernel(oq_ref, w_ref, att_ref, dq_ref, gp_ref):
    for base, ref in ((0, att_ref), (1, dq_ref)):
        put(
            ref,
            [oq_ref[h, base * 128 : (base + 1) * 128, :] for h in range(HEADS)],
            [oq_ref[h, 256 + base * 64 : 320 + base * 64, :].astype(F32) for h in range(HEADS)],
        )
    whi, wmid, _ = split3(w_ref[...])
    wrows = jnp.concatenate([whi.astype(F32), wmid.astype(F32), whi.astype(F32)], axis=0)
    wrows = jnp.concatenate([wrows, jnp.zeros((4, 128), F32)], axis=0).astype(BF)
    blocks = [oq_ref[h, 384:400, :].astype(F32) for h in range(HEADS)]
    zero = jnp.zeros((4, 128), F32)
    for i in range(PROW):
        hi = jnp.concatenate([b[i : i + 1] for b in blocks], axis=0)
        lo = jnp.concatenate([b[8 + i : 9 + i] for b in blocks], axis=0)
        grads = jnp.concatenate([hi, hi, lo, zero], axis=0)
        gp_ref[i] = nn(grads.T.astype(BF), wrows).astype(BF)


def key_kernel(x_ref, in0, in1, in2, in3, far_ref, dk_ref, dv_ref, gw_ref, staged):
    gw_ref[...] = jnp.sum(far_ref[...], axis=0)
    for k, ref in enumerate((in0, in1, in2, in3)):
        staged[lax.rem(x_ref[0] + XS - k, XS)] = ref[...]
    for base, ref in ((0, dk_ref), (1, dv_ref)):
        put(
            ref,
            [staged[h, base * 128 : (base + 1) * 128, :] for h in range(HEADS)],
            [staged[h, 256 + base * 64 : 320 + base * 64, :].astype(F32) for h in range(HEADS)],
        )


def shape(*dims, dtype=BF):
    return jax.ShapeDtypeStruct(dims, dtype)


def call(kernel, out_shape, args, scratch=(), flops=0, moved=0, smem=0, hbm=0, limit=32):
    single = not isinstance(out_shape, tuple)
    rest = len(args) - smem - hbm
    return pl.pallas_call(
        kernel,
        out_shape=out_shape,
        in_specs=[SMEM] * smem + [ANY] * hbm + [VMEM] * rest,
        out_specs=VMEM if single else (VMEM,) * len(out_shape),
        scratch_shapes=list(scratch),
        cost_estimate=pl.CostEstimate(flops=flops, bytes_accessed=moved, transcendentals=0),
        compiler_params=pltpu.CompilerParams(vmem_limit_bytes=limit * 1024 * 1024),
    )(*args)


def prepare(*args):
    return call(
        prepare_kernel,
        (
            shape(HALF, 512), shape(HALF, 256), shape(QROWS, 512), shape(QROWS, 256),
            shape(HALF, QROWS, dtype=F32), shape(8, QROWS, dtype=F32), shape(8, QROWS, dtype=F32),
            shape(256, QROWS, dtype=F32),
        ),
        args,
        smem=1,
        flops=3 * QROWS * KROWS * 256,
        moved=6_000_000,
        limit=PREP,
    )


def attention(*args):
    return call(
        attn_kernel,
        (shape(8, 384, 128), shape(8, 384, 128), shape(XS, 400, 128)),
        args,
        smem=2,
        scratch=(
            pltpu.VMEM((HALF, 512), BF),
            pltpu.VMEM((HALF, 256), BF),
            pltpu.VMEM((HALF, QROWS), F32),
            pltpu.VMEM((256, QROWS), F32),
            pltpu.VMEM((PAIRS, QROWS), F32),
        ),
        flops=13 * QROWS * KROWS * 256,
        moved=8_000_000,
        limit=28,
    )


def seq_index(x, z, c):
    return (x * ZS + z) * CS + c


def body(dp, queries, keys, values, cotangent, pair, pair_weight):
    xz_groups = [[seq_index(x, z, c) for x in range(XS) for z in range(ZS)] for c in range(CS)]
    x_groups = [[seq_index(x, z, c) for x in range(XS)] for z in range(ZS) for c in range(CS)]
    xc_groups = [[seq_index(x, z, c) for x in range(XS) for c in range(CS)] for z in range(ZS)]
    far_groups = [
        [d * 16 + seq_index(x, z, c) for d in range(dp) for z in range(ZS)]
        for x in range(XS)
        for c in range(CS)
    ]
    across = [
        (seq_index(x, z, c), seq_index(x, 1 - z, c))
        for x in range(XS)
        for z in range(ZS)
        for c in range(CS)
    ]
    swap = [(s, s ^ 1) for s in range(16)]

    def ring(k):
        return [
            (seq_index(x, z, c), seq_index((x + k) % XS, z, c))
            for x in range(XS)
            for z in range(ZS)
            for c in range(CS)
        ]

    place = lax.axis_index("seq").astype(jnp.int32)
    core = (place % CS).reshape(1)
    own_z = (place // CS % ZS).reshape(1)
    own_x = (place // (ZS * CS)).reshape(1)
    pair_rows = pair[0]
    kv = call(
        pack_kv_kernel,
        shape(8, 384, 128),
        (keys[0], values[0]),
        hbm=2,
        scratch=(pltpu.VMEM((TOK, 768), BF), pltpu.VMEM((TOK, 768), BF), pltpu.SemaphoreType.DMA((2,))),
        moved=1_500_000,
        limit=56,
    )
    kv, query_rows, cot_rows = lax.optimization_barrier((kv, queries[0], cotangent[0]))
    kv_own = lax.all_to_all(kv, "seq", 0, 0, axis_index_groups=xz_groups)
    qd = call(
        pack_qd_kernel,
        (shape(400, 128),) * XS,
        (own_x, query_rows, cot_rows, pair_rows, pair_weight.T),
        smem=1,
        hbm=4,
        scratch=(
            pltpu.VMEM((TOK, 768), BF),
            pltpu.VMEM((TOK, 768), BF),
            pltpu.VMEM((PROW, PAIRS, 128), BF),
            pltpu.VMEM((HEADS, 128), F32),
            pltpu.VMEM((HEADS, 400, 128), BF),
            pltpu.SemaphoreType.DMA((4,)),
        ),
        flops=2 * 24 * 1024 * 128,
        moved=1_500_000,
        limit=8,
    )
    qd = [qd[0]] + [lax.ppermute(qd[k], "seq", ring(k)) for k in range(1, XS)]
    kv_own, qd = lax.optimization_barrier((kv_own, qd))
    kv_other = lax.ppermute(kv_own, "seq", swap)
    ready = prepare(core, *qd, kv_own)
    dkv_own, dkv_other, oq = attention(core, own_x, kv_other, *ready)
    oq = lax.all_to_all(oq, "seq", 0, 0, axis_index_groups=x_groups)
    dkv_swapped = lax.ppermute(dkv_other, "seq", swap)
    send, keep = call(
        cores_kernel,
        (shape(XS, 384, 128), shape(XS, 384, 128, dtype=F32)),
        (own_z, dkv_own, dkv_swapped),
        smem=1,
        moved=2_400_000,
        limit=8,
    )
    come = lax.ppermute(send, "seq", across)
    total = call(
        weight_kernel, shape(XS * CS, HEADS, 128, dtype=F32), (oq, pair_rows),
        flops=2 * 1024 * 128 * 8, moved=500_000, limit=8,
    )
    total = lax.all_to_all(total, "seq", 0, 0, axis_index_groups=xc_groups).sum(axis=0)
    total, keep = lax.optimization_barrier((total, keep))
    far = jnp.broadcast_to(total[None], (len(far_groups[0]), HEADS, 128))
    far = lax.all_to_all(far, ("dp", "seq"), 0, 0, axis_index_groups=far_groups)
    att, dq, gp = call(
        query_kernel,
        (shape(128, 768), shape(128, 768), shape(PROW, PAIRS, 128)),
        (oq, pair_weight.T),
        flops=2 * 1024 * 128 * 16,
        moved=1_100_000,
        limit=8,
    )
    dkv = call(
        merge_kernel,
        (shape(384, 128),) * XS,
        (own_x, keep, come),
        smem=1,
        moved=1_600_000,
        limit=8,
    )
    dkv = [dkv[0]] + [lax.ppermute(dkv[k], "seq", ring(k)) for k in range(1, XS)]
    dk, dv, gw = call(
        key_kernel,
        (shape(128, 768), shape(128, 768), shape(HEADS, 128, dtype=F32)),
        (own_x, *dkv, far),
        smem=1,
        scratch=(pltpu.VMEM((HEADS, 384, 128), BF),),
        moved=800_000,
        limit=8,
    )
    return att[None], dq[None], dk[None], dv[None], gp[None], gw.T


def solution(mesh):
    rows = P("dp", "seq", None)
    cells = P("dp", "seq", None, None)
    return jax.shard_map(
        functools.partial(body, mesh.shape["dp"]),
        mesh=mesh,
        in_specs=(rows, rows, rows, rows, cells, P()),
        out_specs=(rows, rows, rows, rows, cells, P()),
        check_vma=False,
    )
```

```python
import functools
import math

import jax
import jax.numpy as jnp
from jax import lax
from jax.experimental import pallas as pl
from jax.experimental.pallas import tpu as pltpu
from jax.sharding import PartitionSpec as P

HEADS = 4
HDIM = 192
TOK = 128
POOL = 16
PROW = TOK // POOL
PAIRS = 128
XS = 4
ZS = 2
CS = 2
QROWS = XS * TOK
KROWS = XS * ZS * CS * TOK
HALF = KROWS // CS
PREP = 36
SCALE = HDIM ** (-0.5)
LOG2E = 1.0 / math.log(2.0)
BF = jnp.bfloat16
F32 = jnp.float32
VMEM = pl.BlockSpec(memory_space=pltpu.VMEM)
SMEM = pl.BlockSpec(memory_space=pltpu.SMEM)
ANY = pl.BlockSpec(memory_space=pl.ANY)

FULL_TILE = (0, 2, 3, 5)
HALF_TILE = (1, 1, 4, 4)


def nn(a, b):
    return lax.dot_general(a, b, (((1,), (0,)), ((), ())), preferred_element_type=F32)


def nt(a, b):
    return lax.dot_general(a, b, (((1,), (1,)), ((), ())), preferred_element_type=F32)


def tn(a, b):
    return lax.dot_general(a, b, (((0,), (0,)), ((), ())), preferred_element_type=F32)


def roll_half(x):
    return pltpu.roll(x, 64, 1)


def low_lanes(rows):
    return lax.broadcasted_iota(jnp.int32, (rows, 128), 1) < 64


def split2(x):
    hi = x.astype(BF)
    return hi, (x - hi.astype(F32)).astype(BF)


def split3(x):
    hi = x.astype(BF)
    rest = x - hi.astype(F32)
    mid = rest.astype(BF)
    return hi, mid, (rest - mid.astype(F32)).astype(BF)


def pack_heads(ref):
    low = low_lanes(64)
    for pair in range(2):
        tile = ref[:, (3 * pair + 1) * 128 : (3 * pair + 2) * 128].astype(F32)
        top, bottom = tile[:64], tile[64:]
        even = jnp.where(low, top, roll_half(bottom)).astype(BF)
        odd = jnp.where(low, roll_half(top), bottom).astype(BF)
        for parity, half in ((0, even), (1, odd)):
            head = 2 * pair + parity
            full = FULL_TILE[head]
            yield head, ref[:, full * 128 : (full + 1) * 128], half


def pack_kv_kernel(k_hbm, v_hbm, kv_ref, k_vmem, v_vmem, sems):
    copies = [
        pltpu.make_async_copy(k_hbm, k_vmem, sems.at[0]),
        pltpu.make_async_copy(v_hbm, v_vmem, sems.at[1]),
    ]
    for copy in copies:
        copy.start()
    for base, copy, ref in ((0, copies[0], k_vmem), (1, copies[1], v_vmem)):
        copy.wait()
        for head, full, half in pack_heads(ref):
            for zs in range(ZS):
                slot = head * ZS + zs
                kv_ref[slot, base * 128 : (base + 1) * 128, :] = full
                kv_ref[slot, 256 + base * 64 : 320 + base * 64, :] = half


def pack_qd_kernel(
    x_ref, q_hbm, c_hbm, pair_hbm, w_hbm, out0, out1, out2, out3,
    q_vmem, c_vmem, pair_vmem, w_vmem, staged, sems,
):
    copies = [
        pltpu.make_async_copy(q_hbm, q_vmem, sems.at[0]),
        pltpu.make_async_copy(c_hbm, c_vmem, sems.at[1]),
        pltpu.make_async_copy(w_hbm, w_vmem, sems.at[2]),
        pltpu.make_async_copy(pair_hbm, pair_vmem, sems.at[3]),
    ]
    for copy in copies:
        copy.start()
    for base, copy, ref in ((0, copies[0], q_vmem), (1, copies[1], c_vmem)):
        copy.wait()
        for head, full, half in pack_heads(ref):
            staged[head, base * 128 : (base + 1) * 128, :] = full
            staged[head, 256 + base * 64 : 320 + base * 64, :] = half
    copies[2].wait()
    copies[3].wait()
    wt = weight_rows(w_vmem[...])
    parts = jnp.concatenate([p.astype(F32) for p in split3(wt)], axis=0).astype(BF)
    pair = pair_vmem[...].reshape(PROW * PAIRS, 128)
    prod = nt(parts, pair)
    bias = (prod[0:8] + (prod[8:16] + prod[16:24])) * (1.0 / SCALE)
    for head in range(HEADS):
        rows = jnp.concatenate(
            [bias[head : head + 1, i * 128 : (i + 1) * 128] for i in range(PROW)], axis=0
        )
        hi = rows.astype(BF).astype(F32)
        staged[head, 384:400, :] = jnp.concatenate([hi, rows - hi], axis=0).astype(BF)
    x = x_ref[0]
    for k, out in enumerate((out0, out1, out2, out3)):
        out[...] = staged[lax.rem(x + k, XS)]


def weight_rows(weight):
    return jnp.concatenate([weight, jnp.zeros((4, 128), F32)], axis=0)


def unpack(full, half, rows_low):
    half = half.astype(F32)
    top = jnp.where(rows_low, half, 0.0)
    bottom = jnp.where(rows_low, roll_half(half), 0.0)
    other = jnp.concatenate([top, bottom], axis=0).astype(BF)
    return full, other


def pack_out(block):
    rest = block[:, 128:]
    return block[:, :128].astype(BF), (rest[:64] + roll_half(rest[64:])).astype(BF)


def unpack_keys(kv_ref, mine, ke, vs):
    low = low_lanes(64)
    for m in range(8):
        rows = slice(m * 128, (m + 1) * 128)
        full, other = unpack(kv_ref[m, 0:128, :], kv_ref[m, 256:320, :], low)
        ke[rows, 0:128] = full
        ke[rows, 128:256] = other
        full, other = unpack(kv_ref[m, 128:256, :], kv_ref[m, 320:384, :], low)
        vs[rows, 0:128] = full
        vs[rows, 128:256] = other
    row = lax.broadcasted_iota(jnp.int32, (HALF, 128), 0)
    col = lax.broadcasted_iota(jnp.int32, (HALF, 128), 1)
    cell = lax.shift_right_logical(row, 7) * 16 + mine * 8 + (lax.shift_right_logical(row, 4) & 7)
    table = jnp.where(cell == col, 1.0, 0.0).astype(BF)
    ke[:, 256:384] = table
    ke[:, 384:512] = table


def soften(ke, vs, qe, st):
    s = nt(ke[...], qe[...])
    top = jnp.max(jnp.max(s.reshape(HALF // 8, 8, QROWS), axis=0), axis=0, keepdims=True)
    top = top * (SCALE * LOG2E)
    w = jnp.exp2(s * (SCALE * LOG2E) - top)
    st[...] = w
    total = jnp.sum(w.reshape(HALF // 8, 8, QROWS), axis=0)
    return top, total, tn(vs[...], w.astype(BF))


def prepare_kernel(
    core_ref, qd0, qd1, qd2, qd3, kv_own, ke, vs, qe, cs, st, top_ref, total_ref, ot_ref
):
    low = low_lanes(64)
    unpack_keys(kv_own, core_ref[0], ke, vs)
    for k, qd_ref in enumerate((qd0, qd1, qd2, qd3)):
        base = k * 128
        full, other = unpack(qd_ref[0:128, :], qd_ref[256:320, :], low)
        qe[base : base + 128, 0:128] = full
        qe[base : base + 128, 128:256] = other
        full, other = unpack(qd_ref[128:256, :], qd_ref[320:384, :], low)
        cs[base : base + 128, 0:128] = full
        cs[base : base + 128, 128:256] = other
        rows = qd_ref[384:400, :].astype(F32)
        for part in range(2):
            wide = jnp.broadcast_to(rows[part * 8 : part * 8 + 8, None, :], (8, POOL, 128))
            qe[base : base + 128, 256 + part * 128 : 384 + part * 128] = wide.reshape(128, 128).astype(BF)
    top, total_ref[...], ot_ref[...] = soften(ke, vs, qe, st)
    top_ref[...] = jnp.broadcast_to(top, top_ref.shape)


def attn_kernel(
    core_ref, x_ref, kv_other, ke_own, vs_own, qe, cs, st_own, top_ref, total_ref, ot_ref,
    dko_ref, dkx_ref, oq_ref, ke_other, vs_other, st_other, dqt, pool,
):
    core = core_ref[0]
    unpack_keys(kv_other, 1 - core, ke_other, vs_other)
    top_other, total_other, ot_other = soften(ke_other, vs_other, qe, st_other)
    top_own = top_ref[0:1, :]
    top = jnp.maximum(top_own, top_other)
    own, other = jnp.exp2(top_own - top), jnp.exp2(top_other - top)
    total = total_ref[...] * own + total_other * other
    inv = 1.0 / jnp.sum(total, axis=0, keepdims=True)
    halves = (
        (ke_own, vs_own, st_own, own * inv, core, dko_ref),
        (ke_other, vs_other, st_other, other * inv, 1 - core, dkx_ref),
    )
    ot = ot_ref[...] * own + ot_other * other
    att = (ot * inv).astype(BF).astype(F32)
    delta = jnp.sum(att * cs[...].astype(F32).T, axis=0, keepdims=True)
    att = att.T
    for half, (ke, vs, st, share, mine, ref) in enumerate(halves):
        prob = st[...] * share
        dv = nn(prob.astype(BF), cs[...])
        ds = prob * (nt(vs[...], cs[...]) - delta)
        low_ds = ds.astype(BF)
        dk = nn(low_ds, qe[:, 0:256]) * SCALE
        part = tn(ke[:, 0:256], low_ds)
        dqt[...] = part if half == 0 else dqt[...] + part
        pooled = jnp.sum(ds.reshape(HALF // POOL, POOL, QROWS), axis=1)
        for m in range(8):
            rows = slice(m * 128, (m + 1) * 128)
            full, rest = pack_out(dk[rows])
            ref[m, 0:128, :] = full
            ref[m, 256:320, :] = rest
            full, rest = pack_out(dv[rows])
            ref[m, 128:256, :] = full
            ref[m, 320:384, :] = rest
            pool[pl.ds(pl.multiple_of(m * 16 + mine * 8, 8), 8), :] = pooled[m * 8 : m * 8 + 8]

    row = lax.broadcasted_iota(jnp.int32, (QROWS // POOL, QROWS), 0)
    col = lax.broadcasted_iota(jnp.int32, (QROWS // POOL, QROWS), 1)
    pick = jnp.where(row == lax.shift_right_logical(col, 4), 1.0, 0.0).astype(BF)
    hi, lo = split2(pool[...])
    grad_bias = nt(pick, hi) + nt(pick, lo)
    dq = dqt[...].T * SCALE
    for k in range(XS):
        to = lax.rem(x_ref[0] + XS - k, XS)
        at = slice(k * 128, (k + 1) * 128)
        full, rest = pack_out(att[at])
        oq_ref[to, 0:128, :] = full
        oq_ref[to, 256:320, :] = rest
        full, rest = pack_out(dq[at])
        oq_ref[to, 128:256, :] = full
        oq_ref[to, 320:384, :] = rest
        rows = grad_bias[k * PROW : (k + 1) * PROW]
        hi = rows.astype(BF).astype(F32)
        oq_ref[to, 384:400, :] = jnp.concatenate([hi, rows - hi], axis=0).astype(BF)


def weight_kernel(oq_ref, pair_ref, out_ref):
    rows = []
    for part in range(2):
        for head in range(HEADS):
            block = oq_ref[head, 384:400, :].astype(F32)[part * 8 : part * 8 + 8]
            rows.append(jnp.concatenate([block[i : i + 1] for i in range(PROW)], axis=1))
    prod = nn(jnp.concatenate(rows, axis=0).astype(BF), pair_ref[...].reshape(PROW * PAIRS, 128))
    out_ref[...] = jnp.broadcast_to((prod[0:4] + prod[4:8])[None], out_ref.shape)


def spread_kernel(near_ref, out_ref):
    total = jnp.sum(near_ref[...], axis=0)
    out_ref[...] = jnp.broadcast_to(total[None], out_ref.shape)


def cores_kernel(z_ref, own_ref, other_ref, send_ref, keep_ref):
    z = z_ref[0]
    for x in range(XS):
        away = x * ZS + 1 - z
        send_ref[x] = (own_ref[away].astype(F32) + other_ref[away].astype(F32)).astype(BF)
        here = x * ZS + z
        keep_ref[x] = own_ref[here].astype(F32) + other_ref[here].astype(F32)


def merge_kernel(x_ref, keep_ref, come_ref, out0, out1, out2, out3):
    for k, out in enumerate((out0, out1, out2, out3)):
        to = lax.rem(x_ref[0] + k, XS)
        out[...] = (keep_ref[to] + come_ref[to].astype(F32)).astype(BF)


def put(ref, fulls, halves):
    low = low_lanes(64)
    for pair in range(2):
        even, odd = halves[2 * pair], halves[2 * pair + 1]
        mid = jnp.concatenate(
            [jnp.where(low, even, roll_half(odd)), jnp.where(low, roll_half(even), odd)], axis=0
        )
        ref[:, (3 * pair) * 128 : (3 * pair + 1) * 128] = fulls[2 * pair].astype(BF)
        ref[:, (3 * pair + 1) * 128 : (3 * pair + 2) * 128] = mid.astype(BF)
        ref[:, (3 * pair + 2) * 128 : (3 * pair + 3) * 128] = fulls[2 * pair + 1].astype(BF)


def query_kernel(oq_ref, w_ref, att_ref, dq_ref, gp_ref):
    for base, ref in ((0, att_ref), (1, dq_ref)):
        put(
            ref,
            [oq_ref[h, base * 128 : (base + 1) * 128, :] for h in range(HEADS)],
            [oq_ref[h, 256 + base * 64 : 320 + base * 64, :].astype(F32) for h in range(HEADS)],
        )
    whi, wmid, _ = split3(w_ref[...])
    wrows = jnp.concatenate([whi.astype(F32), wmid.astype(F32), whi.astype(F32)], axis=0)
    wrows = jnp.concatenate([wrows, jnp.zeros((4, 128), F32)], axis=0).astype(BF)
    blocks = [oq_ref[h, 384:400, :].astype(F32) for h in range(HEADS)]
    zero = jnp.zeros((4, 128), F32)
    for i in range(PROW):
        hi = jnp.concatenate([b[i : i + 1] for b in blocks], axis=0)
        lo = jnp.concatenate([b[8 + i : 9 + i] for b in blocks], axis=0)
        grads = jnp.concatenate([hi, hi, lo, zero], axis=0)
        gp_ref[i] = nn(grads.T.astype(BF), wrows).astype(BF)


def key_kernel(x_ref, in0, in1, in2, in3, far_ref, dk_ref, dv_ref, gw_ref, staged):
    gw_ref[...] = jnp.sum(far_ref[...], axis=0)
    for k, ref in enumerate((in0, in1, in2, in3)):
        staged[lax.rem(x_ref[0] + XS - k, XS)] = ref[...]
    for base, ref in ((0, dk_ref), (1, dv_ref)):
        put(
            ref,
            [staged[h, base * 128 : (base + 1) * 128, :] for h in range(HEADS)],
            [staged[h, 256 + base * 64 : 320 + base * 64, :].astype(F32) for h in range(HEADS)],
        )


def shape(*dims, dtype=BF):
    return jax.ShapeDtypeStruct(dims, dtype)


def call(kernel, out_shape, args, scratch=(), flops=0, moved=0, smem=0, hbm=0, limit=32):
    single = not isinstance(out_shape, tuple)
    rest = len(args) - smem - hbm
    return pl.pallas_call(
        kernel,
        out_shape=out_shape,
        in_specs=[SMEM] * smem + [ANY] * hbm + [VMEM] * rest,
        out_specs=VMEM if single else (VMEM,) * len(out_shape),
        scratch_shapes=list(scratch),
        cost_estimate=pl.CostEstimate(flops=flops, bytes_accessed=moved, transcendentals=0),
        compiler_params=pltpu.CompilerParams(vmem_limit_bytes=limit * 1024 * 1024),
    )(*args)


def prepare(*args):
    return call(
        prepare_kernel,
        (
            shape(HALF, 512), shape(HALF, 256), shape(QROWS, 512), shape(QROWS, 256),
            shape(HALF, QROWS, dtype=F32), shape(8, QROWS, dtype=F32), shape(8, QROWS, dtype=F32),
            shape(256, QROWS, dtype=F32),
        ),
        args,
        smem=1,
        flops=3 * QROWS * KROWS * 256,
        moved=6_000_000,
        limit=PREP,
    )


def attention(*args):
    return call(
        attn_kernel,
        (shape(8, 384, 128), shape(8, 384, 128), shape(XS, 400, 128)),
        args,
        smem=2,
        scratch=(
            pltpu.VMEM((HALF, 512), BF),
            pltpu.VMEM((HALF, 256), BF),
            pltpu.VMEM((HALF, QROWS), F32),
            pltpu.VMEM((256, QROWS), F32),
            pltpu.VMEM((PAIRS, QROWS), F32),
        ),
        flops=13 * QROWS * KROWS * 256,
        moved=8_000_000,
        limit=28,
    )


def seq_index(x, z, c):
    return (x * ZS + z) * CS + c


def body(dp, queries, keys, values, cotangent, pair, pair_weight):
    xz_groups = [[seq_index(x, z, c) for x in range(XS) for z in range(ZS)] for c in range(CS)]
    x_groups = [[seq_index(x, z, c) for x in range(XS)] for z in range(ZS) for c in range(CS)]
    xc_groups = [[seq_index(x, z, c) for x in range(XS) for c in range(CS)] for z in range(ZS)]
    far_groups = [
        [d * 16 + seq_index(x, z, c) for d in range(dp) for z in range(ZS)]
        for x in range(XS)
        for c in range(CS)
    ]
    across = [
        (seq_index(x, z, c), seq_index(x, 1 - z, c))
        for x in range(XS)
        for z in range(ZS)
        for c in range(CS)
    ]
    swap = [(s, s ^ 1) for s in range(16)]

    def ring(k):
        return [
            (seq_index(x, z, c), seq_index((x + k) % XS, z, c))
            for x in range(XS)
            for z in range(ZS)
            for c in range(CS)
        ]

    place = lax.axis_index("seq").astype(jnp.int32)
    core = (place % CS).reshape(1)
    own_z = (place // CS % ZS).reshape(1)
    own_x = (place // (ZS * CS)).reshape(1)
    pair_rows = pair[0]
    kv = call(
        pack_kv_kernel,
        shape(8, 384, 128),
        (keys[0], values[0]),
        hbm=2,
        scratch=(pltpu.VMEM((TOK, 768), BF), pltpu.VMEM((TOK, 768), BF), pltpu.SemaphoreType.DMA((2,))),
        moved=1_500_000,
        limit=56,
    )
    kv, query_rows, cot_rows = lax.optimization_barrier((kv, queries[0], cotangent[0]))
    kv_own = lax.all_to_all(kv, "seq", 0, 0, axis_index_groups=xz_groups)
    qd = call(
        pack_qd_kernel,
        (shape(400, 128),) * XS,
        (own_x, query_rows, cot_rows, pair_rows, pair_weight.T),
        smem=1,
        hbm=4,
        scratch=(
            pltpu.VMEM((TOK, 768), BF),
            pltpu.VMEM((TOK, 768), BF),
            pltpu.VMEM((PROW, PAIRS, 128), BF),
            pltpu.VMEM((HEADS, 128), F32),
            pltpu.VMEM((HEADS, 400, 128), BF),
            pltpu.SemaphoreType.DMA((4,)),
        ),
        flops=2 * 24 * 1024 * 128,
        moved=1_500_000,
        limit=8,
    )
    qd = [qd[0]] + [lax.ppermute(qd[k], "seq", ring(k)) for k in range(1, XS)]
    kv_own, qd = lax.optimization_barrier((kv_own, qd))
    kv_other = lax.ppermute(kv_own, "seq", swap)
    ready = prepare(core, *qd, kv_own)
    dkv_own, dkv_other, oq = attention(core, own_x, kv_other, *ready)
    oq = lax.all_to_all(oq, "seq", 0, 0, axis_index_groups=x_groups)
    dkv_swapped = lax.ppermute(dkv_other, "seq", swap)
    send, keep = call(
        cores_kernel,
        (shape(XS, 384, 128), shape(XS, 384, 128, dtype=F32)),
        (own_z, dkv_own, dkv_swapped),
        smem=1,
        moved=2_400_000,
        limit=8,
    )
    come = lax.ppermute(send, "seq", across)
    total = call(
        weight_kernel, shape(XS * CS, HEADS, 128, dtype=F32), (oq, pair_rows),
        flops=2 * 1024 * 128 * 8, moved=500_000, limit=8,
    )
    total = lax.all_to_all(total, "seq", 0, 0, axis_index_groups=xc_groups)
    total, keep = lax.optimization_barrier((total, keep))
    far = call(
        spread_kernel, shape(len(far_groups[0]), HEADS, 128, dtype=F32), (total,),
        moved=150_000, limit=8,
    )
    far = lax.all_to_all(far, ("dp", "seq"), 0, 0, axis_index_groups=far_groups)
    att, dq, gp = call(
        query_kernel,
        (shape(128, 768), shape(128, 768), shape(PROW, PAIRS, 128)),
        (oq, pair_weight.T),
        flops=2 * 1024 * 128 * 16,
        moved=1_100_000,
        limit=8,
    )
    dkv = call(
        merge_kernel,
        (shape(384, 128),) * XS,
        (own_x, keep, come),
        smem=1,
        moved=1_600_000,
        limit=8,
    )
    dkv = [dkv[0]] + [lax.ppermute(dkv[k], "seq", ring(k)) for k in range(1, XS)]
    dk, dv, gw = call(
        key_kernel,
        (shape(128, 768), shape(128, 768), shape(HEADS, 128, dtype=F32)),
        (own_x, *dkv, far),
        smem=1,
        scratch=(pltpu.VMEM((HEADS, 384, 128), BF),),
        moved=800_000,
        limit=8,
    )
    return att[None], dq[None], dk[None], dv[None], gp[None], gw.T


def solution(mesh):
    rows = P("dp", "seq", None)
    cells = P("dp", "seq", None, None)
    return jax.shard_map(
        functools.partial(body, mesh.shape["dp"]),
        mesh=mesh,
        in_specs=(rows, rows, rows, rows, cells, P()),
        out_specs=(rows, rows, rows, rows, cells, P()),
        check_vma=False,
    )
```
